256 devices in a mesh: dp: 8 (over z), zone: 32 (over x, y, core).
Axes of the slice: x: 4, y: 4, z: 8, core: 2. Of those that a mesh axis runs over, the one named last changes fastest.
Arguments:
- features: bfloat16 [8, 4096, 4096], P('dp', 'zone'), may hold values from -6 to 6
- query_states: bfloat16 [8, 4096, 4096], P('dp', 'zone'), may hold values from -160 to 160
- key_states: bfloat16 [8, 4096, 4096], P('dp', 'zone'), may hold values from -8 to 8
- value_states: bfloat16 [8, 4096, 4096], P('dp', 'zone'), may hold values from -6 to 6
- cotangent: bfloat16 [8, 4096, 4096], P('dp', 'zone'), may hold values from -144 to 144
- adapter_down: bfloat16 [2, 64, 4096], replicated, may hold values from -0.09375 to 0.09375
- adapter_up: bfloat16 [2, 64, 4096], replicated, may hold values from -0.09375 to 0.09375
- block_lists: int32 [8, 64, 8], P('dp', 'zone'), may hold values from 0 to 63, all different within a row
- block_counts: int32 [8, 64], P('dp', 'zone'), may hold values from 2 to 8
Outputs:
- query_grad: bfloat16 [8, 4096, 4096], P('dp', 'zone')
- key_grad: bfloat16 [8, 4096, 4096], P('dp', 'zone')
- value_grad: bfloat16 [8, 4096, 4096], P('dp', 'zone')
- down_grad: float32 [2, 64, 4096], P(None, None, 'zone')
- up_grad: float32 [2, 64, 4096], P(None, None, 'zone')
The draws below stay inside these ranges and needn't reach their ends.
Inputs may be any that keep to these rules, and one draw needn't show every extreme that they name: `block_lists`: each block's 8 entries are different blocks of its window, possibly itself; only the first block_counts entries are read.
All inputs are finite; a program needn't handle non-finite values.
Results may differ from the reference program's by a relative error of at most 0.0074.
Values may be sent and summed in bfloat16 or wider, within the bound.
No kernel may reach another device: no remote copies, remote signals or barrier semaphores. Data moves between devices by JAX's collectives and lax.ppermute only.
A program may use at most 64 MiB of HBM per device.

```python
import math
import jax
import jax.numpy as jnp
from jax import lax

D = 4096
HEADS = 32
HEAD = 128
HD = 4096
BLK = 64
NBR = 8
RANK = 64
WINDOWS = 8
NBLK = 64
ZONES = 4096


def shared_keys(key):
    return jax.random.normal(jax.random.fold_in(key, 101), (WINDOWS, ZONES, HD), jnp.float32)


def draw_key_states(key, part):
    base = shared_keys(key)
    return jnp.clip(base, -8.0, 8.0).astype(jnp.bfloat16)


def draw_query_states(key, part):
    base = jnp.clip(shared_keys(key), -8.0, 8.0)
    key = jax.random.fold_in(key, 11)
    noise = jnp.clip(jax.random.normal(key, base.shape, jnp.float32), -8.0, 8.0)
    return noise.astype(jnp.bfloat16)


def set_ends(array, key, least, high):
    place = [jax.random.randint(jax.random.fold_in(key, axis), (), 0, length) for axis, length in enumerate(array.shape)]
    widest = array.shape.index(max(array.shape))
    next_to = place[:widest] + [(place[widest] + 1) % array.shape[widest]] + place[widest + 1:]
    return array.at[tuple(place)].set(least).at[tuple(next_to)].set(high)


def raised(result, own_key, source, target, blocks, factor):
    def block_of(dim):
        return (jnp.arange(result.shape[dim]) // (result.shape[dim] // blocks)).reshape((-1,) + (1,) * (result.ndim - 1 - dim))

    near = jax.random.permutation(own_key, blocks)[block_of(target)]
    second = (block_of(target) + blocks // 2) % blocks
    return jnp.where((block_of(source) == near) | (block_of(source) == second), factor * result, result)


def block_levels(own_key, extent, shards, low, high):
    factor_of = 1.0
    for axis_at, shards_of in shards:
        steps = jax.random.uniform(jax.random.fold_in(jax.random.fold_in(own_key, 6), axis_at), (shards_of,), jnp.float32, low / len(shards), high / len(shards))
        factor_of = factor_of * jnp.repeat(jnp.exp(steps), extent[axis_at] // shards_of).reshape((-1,) + (1,) * (len(extent) - 1 - axis_at))
    return factor_of


def choose_distinct(key, rows, amount, top, lift):
    ranking = jax.random.permutation(jax.random.fold_in(key, 1), amount)
    favour = ranking
    for power in range(3):
        favour = favour * favour // amount
    favour = favour * lift // amount
    tickets = jax.random.randint(jax.random.fold_in(key, 2), (rows, amount), 0, 4096) + favour
    sure = jax.random.permutation(jax.random.fold_in(key, 3), rows)[jnp.arange(amount) % rows]
    tickets = jnp.where(jnp.arange(rows)[:, None] == sure[None, :], 1 << 14, tickets)
    merit = tickets * amount + jnp.arange(amount)
    return lax.top_k(merit.astype(jnp.int32), top)[1].astype(jnp.int32)


def gaussian(key, dims, spread, limit, shards=(), kind=jnp.bfloat16):
    factor_of = block_levels(key, dims, shards, -0.22, 0.18) if shards else 1.0
    drawn = jax.random.normal(key, dims, jnp.float32) * spread * factor_of
    return jnp.minimum(jnp.maximum(drawn, -limit), limit).astype(kind)


def heavy_noise(stream_key, extent, width, limit, pieces, heavy, held_as=jnp.bfloat16):
    drawn = width * jax.random.normal(stream_key, extent, jnp.float32)
    if pieces:
        drawn = drawn * block_levels(stream_key, extent, pieces, -0.22, 0.18)
    return jnp.clip(raised(drawn, jax.random.fold_in(stream_key, 3), *heavy), -limit, limit).astype(held_as)


def setup_inputs(seed: int = 0) -> dict:
    seeds = jax.random.split(jax.random.key(seed), 10)
    return {
        "features": heavy_noise(seeds[0], (WINDOWS, ZONES, D), 1.0, 6.0, ((0, 8), (1, 32)), (1, 2, 32, 2.75)),
        "query_states": draw_query_states(jax.random.fold_in(seeds[9], 71), 0),
        "key_states": draw_key_states(jax.random.fold_in(seeds[9], 71), 0),
        "value_states": gaussian(seeds[3], (WINDOWS, ZONES, HD), 1.0, 6.0, ((0, 8), (1, 32))),
        "cotangent": gaussian(seeds[4], (WINDOWS, ZONES, HD), 24.0, 144.0, ((0, 8), (1, 32))),
        "adapter_down": gaussian(seeds[5], (2, RANK, D), D ** -0.5, 0.09375),
        "adapter_up": gaussian(seeds[6], (2, RANK, HD), HD ** -0.5, 0.09375),
        "block_lists": choose_distinct(seeds[7], WINDOWS * NBLK, NBLK, NBR, 2048).reshape((WINDOWS, NBLK, NBR)),
        "block_counts": set_ends(jax.random.randint(seeds[8], (WINDOWS, NBLK), 2, NBR + 1), jax.random.fold_in(seeds[8], 1), 2, NBR).astype(jnp.int32),
    }


def head_backward(query_head, key_head, value_head, grad_head, slot_ids, slot_valid):
    scale = HEAD ** (-0.5)
    query_f = query_head.astype(jnp.float32)
    key_f = key_head[slot_ids].astype(jnp.float32)
    value_f = value_head[slot_ids].astype(jnp.float32)
    grad_f = grad_head.astype(jnp.float32)
    scores = jnp.einsum('bid,bskd->bisk', query_f, key_f) * scale
    scores = jnp.where(slot_valid[:, None, :, None], scores, -jnp.inf)
    highest = lax.optimization_barrier(jnp.max(scores, axis=(2, 3), keepdims=True))
    expd = jnp.exp(scores - highest)
    weights = expd / lax.optimization_barrier(jnp.sum(expd, axis=(2, 3), keepdims=True))
    weights_b = lax.optimization_barrier(weights.astype(jnp.bfloat16))
    weights_f = weights_b.astype(jnp.float32)
    attended = jnp.einsum('bisk,bskd->bid', weights_f, value_f)
    delta = lax.optimization_barrier(jnp.sum(grad_f * attended, axis=-1))
    grad_weights = jnp.einsum('bid,bskd->bisk', grad_f, value_f)
    grad_rounded = lax.optimization_barrier((weights * (grad_weights - delta[:, :, None, None])).astype(jnp.bfloat16))
    grad_scores = grad_rounded.astype(jnp.float32)
    query_grad = (jnp.einsum('bisk,bskd->bid', grad_scores, key_f) * scale).astype(jnp.bfloat16)
    key_terms = jnp.einsum('bisk,bid->bskd', grad_scores, query_f) * scale
    value_terms = jnp.einsum('bisk,bid->bskd', weights_f, grad_f)
    flat_ids = slot_ids.reshape(-1)
    key_grad = jax.ops.segment_sum(key_terms.reshape((-1, BLK, HEAD)), flat_ids, num_segments=NBLK)
    value_grad = jax.ops.segment_sum(value_terms.reshape((-1, BLK, HEAD)), flat_ids, num_segments=NBLK)
    return (query_grad, key_grad.astype(jnp.bfloat16), value_grad.astype(jnp.bfloat16))

def by_head(states):
    return states.reshape(NBLK, BLK, HEADS, HEAD).transpose(2, 0, 1, 3)

def by_row(states):
    return states.transpose(1, 2, 0, 3).reshape(ZONES, HD)

def reference(features, query_states, key_states, value_states, cotangent, adapter_down, adapter_up, block_lists, block_counts):
    slot_range = jnp.arange(NBR + 1, dtype=jnp.int32)
    down_total = jnp.zeros((2, RANK, D), jnp.float32)
    up_total = jnp.zeros((2, RANK, HD), jnp.float32)
    query_out = []
    key_out = []
    value_out = []
    for window in range(WINDOWS):
        own_ids = jnp.arange(NBLK, dtype=jnp.int32)[:, None]
        slot_ids = jnp.concatenate([own_ids, block_lists[window].astype(jnp.int32)], axis=1)
        slot_valid = slot_range[None, :] < block_counts[window].astype(jnp.int32)[:, None] + 1

        def one_head(operands):
            return head_backward(operands[0], operands[1], operands[2], operands[3], slot_ids, slot_valid)
        head_grads = lax.map(one_head, (by_head(query_states[window]), by_head(key_states[window]), by_head(value_states[window]), by_head(cotangent[window])))
        query_grad = by_row(head_grads[0])
        key_grad = by_row(head_grads[1])
        value_grad = by_row(head_grads[2])
        query_out.append(query_grad)
        key_out.append(key_grad)
        value_out.append(value_grad)
        stacked = jnp.stack([key_grad, value_grad]).astype(jnp.float32)
        rows_x = features[window].astype(jnp.float32)
        lowrank = jnp.einsum('rd,tad->tra', rows_x, adapter_down.astype(jnp.float32)).astype(jnp.bfloat16)
        up_total = up_total + jnp.einsum('tra,trh->tah', lowrank.astype(jnp.float32), stacked)
        back_low = jnp.einsum('trh,tah->tra', stacked, adapter_up.astype(jnp.float32)).astype(jnp.bfloat16)
        down_total = down_total + jnp.einsum('tra,rd->tad', back_low.astype(jnp.float32), rows_x)
    factor = 1.0 / math.sqrt(WINDOWS * ZONES)
    return (jnp.stack(query_out), jnp.stack(key_out), jnp.stack(value_out), down_total * factor, up_total * factor)
```

```python
import functools
import math

import jax
import jax.numpy as jnp
from jax import lax
from jax.experimental import pallas as pl
from jax.experimental.pallas import tpu as pltpu
from jax.sharding import PartitionSpec as P

HEAD = 128
BLK = 64
VMEM_ALL = 60 << 20
META = 16
BF = jnp.bfloat16
F32 = jnp.float32
NT = (((1,), (1,)), ((), ()))
TN = (((0,), (0,)), ((), ()))
NN = (((1,), (0,)), ((), ()))


def dot(a, b, dims):
    return lax.dot_general(a, b, dims, preferred_element_type=F32)


def whole(shape, space=pltpu.VMEM):
    return pl.BlockSpec(memory_space=space)


def pack_kernel(meta_ref, q_ref, k_ref, v_ref, g_ref, out_ref):
    rows = q_ref.shape[0]
    for j in range(out_ref.shape[0]):
        cols = slice(j * HEAD, (j + 1) * HEAD)
        for t, ref in enumerate((q_ref, k_ref, v_ref, g_ref)):
            out_ref[j, t * rows:(t + 1) * rows, :] = ref[:, cols]
        out_ref[j, 4 * rows:, :] = meta_ref[...]


def pack(meta, q, k, v, g, heads_per_step=8):
    rows, feats = q.shape
    heads = feats // HEAD
    out_rows = 4 * rows + META
    spec = pl.BlockSpec((rows, heads_per_step * HEAD), lambda i: (0, i))
    return pl.pallas_call(
        pack_kernel,
        grid=(heads // heads_per_step,),
        in_specs=[pl.BlockSpec((META, HEAD), lambda i: (0, 0))] + [spec] * 4,
        out_specs=pl.BlockSpec((heads_per_step, out_rows, HEAD), lambda i: (i, 0, 0)),
        out_shape=jax.ShapeDtypeStruct((heads, out_rows, HEAD), BF),
        compiler_params=pltpu.CompilerParams(vmem_limit_bytes=VMEM_ALL),
        cost_estimate=pl.CostEstimate(flops=0, bytes_accessed=16 * rows * feats, transcendentals=0),
        name="pack",
    )(meta, q, k, v, g)


def attention_kernel(ids_ref, counts_ref, states_ref, out_ref, dk_ref, dv_ref, *, rows, slots):
    pairs = out_ref.shape[0]
    stride = 4 * rows + META
    scale = HEAD ** (-0.5)
    dk_ref[...] = jnp.zeros_like(dk_ref)
    dv_ref[...] = jnp.zeros_like(dv_ref)
    first_half = lax.broadcasted_iota(jnp.int32, (1, 2 * BLK), 1) < BLK

    def body(p, carry):
        base = p * stride

        def load(row, n):
            return states_ref[pl.ds(pl.multiple_of(row, 16), n), :]

        def blockdiag(x):
            zero = jnp.zeros((BLK, HEAD), BF)
            return jnp.concatenate(
                [
                    jnp.concatenate([x[:BLK], zero], axis=1),
                    jnp.concatenate([zero, x[BLK:]], axis=1),
                ],
                axis=0,
            )

        q_bd = blockdiag(load(base, rows))
        g_bd = blockdiag(load(base + 3 * rows, rows))
        ids = []
        k_parts = []
        v_parts = []
        for s in range(slots):
            pair_ids = [ids_ref[(2 * p + c) * slots + s] for c in range(2)]
            ids.append(pair_ids)
            at = [(i // 2) * stride + (i % 2) * BLK for i in pair_ids]
            k_parts.append(jnp.concatenate([load(a + rows, BLK) for a in at], axis=1))
            v_parts.append(jnp.concatenate([load(a + 2 * rows, BLK) for a in at], axis=1))
        k_cat = jnp.concatenate(k_parts, axis=0)
        v_cat = jnp.concatenate(v_parts, axis=0)
        count = jnp.where(first_half, counts_ref[2 * p], counts_ref[2 * p + 1])
        slot = lax.broadcasted_iota(jnp.int32, (slots * BLK, 2 * BLK), 0) // BLK
        scores = jnp.where(slot <= count, dot(k_cat, q_bd, NT), -jnp.inf)
        highest = jnp.max(scores, axis=0, keepdims=True)
        expd = jnp.exp((scores - highest) * scale)
        weights = expd * (1.0 / jnp.sum(expd, axis=0, keepdims=True))
        weights_b = weights.astype(BF)
        grad_weights = dot(v_cat, g_bd, NT)
        delta = jnp.sum(weights_b.astype(F32) * grad_weights, axis=0, keepdims=True)
        grad_scores = (weights * (grad_weights - delta)).astype(BF)
        dk = dot(grad_scores, q_bd, NN)
        dv = dot(weights_b, g_bd, NN)
        for s in range(slots):
            for c in range(2):
                at = pl.ds(pl.multiple_of(ids[s][c] * BLK, BLK), BLK)
                part = (slice(s * BLK, (s + 1) * BLK), slice(c * HEAD, (c + 1) * HEAD))
                dk_ref[at, :] += dk[part]
                dv_ref[at, :] += dv[part]
        dq = dot(grad_scores, k_cat, TN)
        out_ref[p, :BLK, :] = (dq[:BLK, :HEAD] * scale).astype(BF)
        out_ref[p, BLK:2 * BLK, :] = (dq[BLK:, HEAD:] * scale).astype(BF)
        return carry

    lax.fori_loop(0, pairs, body, 0)

    def finish(p, carry):
        at = pl.ds(pl.multiple_of(p * rows, rows), rows)
        out_ref[p, rows:2 * rows, :] = (dk_ref[at, :] * scale).astype(BF)
        out_ref[p, 2 * rows:, :] = dv_ref[at, :].astype(BF)
        return carry

    lax.fori_loop(0, pairs, finish, 0)


def attention(ids, counts, states, rows):
    pairs = states.shape[0]
    slots = ids.shape[1]
    all_rows = pairs * rows
    return pl.pallas_call(
        functools.partial(attention_kernel, rows=rows, slots=slots),
        in_specs=[
            pl.BlockSpec(memory_space=pltpu.SMEM),
            pl.BlockSpec(memory_space=pltpu.SMEM),
            pl.BlockSpec(memory_space=pltpu.VMEM),
        ],
        out_specs=pl.BlockSpec(memory_space=pltpu.VMEM),
        out_shape=jax.ShapeDtypeStruct((pairs, 3 * rows, HEAD), BF),
        scratch_shapes=[pltpu.VMEM((all_rows, HEAD), F32), pltpu.VMEM((all_rows, HEAD), F32)],
        compiler_params=pltpu.CompilerParams(vmem_limit_bytes=VMEM_ALL),
        cost_estimate=pl.CostEstimate(
            flops=2 * 5 * all_rows * slots * BLK * HEAD * 2,
            bytes_accessed=states.size * 2 + pairs * 3 * rows * HEAD * 2,
            transcendentals=all_rows * slots * BLK,
        ),
        name="attention",
    )(ids.reshape(-1), counts, states.reshape(-1, HEAD))


def down_kernel(grads_ref, up_ref, x_ref, out_ref):
    heads = grads_ref.shape[0]
    rows, feats = x_ref.shape
    low = []
    for t in range(2):
        total = jnp.zeros((rows, up_ref.shape[1]), F32)
        for h in range(heads):
            part = grads_ref[h, (1 + t) * rows:(2 + t) * rows, :]
            total += dot(part, up_ref[t, :, h * HEAD:(h + 1) * HEAD], NT)
        low.append(total)
    back_low = jnp.concatenate(low, axis=1).astype(BF)
    for h in range(heads):
        out_ref[h] = dot(back_low, x_ref[:, h * HEAD:(h + 1) * HEAD], TN).astype(BF)


def down_terms(grads, adapter_up, x):
    heads = grads.shape[0]
    rows, feats = x.shape
    return pl.pallas_call(
        down_kernel,
        in_specs=[pl.BlockSpec(memory_space=pltpu.VMEM)] * 3,
        out_specs=pl.BlockSpec(memory_space=pltpu.VMEM),
        out_shape=jax.ShapeDtypeStruct((heads, 2 * adapter_up.shape[1], HEAD), BF),
        compiler_params=pltpu.CompilerParams(vmem_limit_bytes=VMEM_ALL),
        cost_estimate=pl.CostEstimate(
            flops=8 * rows * feats * adapter_up.shape[1],
            bytes_accessed=12 * rows * feats,
            transcendentals=0,
        ),
        name="down_terms",
    )(grads, adapter_up, x)


def unpack_kernel(in_ref, q_ref, k_ref, v_ref):
    rows = q_ref.shape[0]
    for j in range(in_ref.shape[0]):
        cols = slice(j * HEAD, (j + 1) * HEAD)
        for t, ref in enumerate((q_ref, k_ref, v_ref)):
            ref[:, cols] = in_ref[j, t * rows:(t + 1) * rows, :]


def unpack(grads, heads_per_step=8):
    heads, rows3, _ = grads.shape
    rows = rows3 // 3
    shape = jax.ShapeDtypeStruct((rows, heads * HEAD), BF)
    spec = pl.BlockSpec((rows, heads_per_step * HEAD), lambda i: (0, i))
    return pl.pallas_call(
        unpack_kernel,
        grid=(heads // heads_per_step,),
        in_specs=[pl.BlockSpec((heads_per_step, rows3, HEAD), lambda i: (i, 0, 0))],
        out_specs=[spec] * 3,
        out_shape=[shape] * 3,
        compiler_params=pltpu.CompilerParams(vmem_limit_bytes=VMEM_ALL),
        cost_estimate=pl.CostEstimate(
            flops=0, bytes_accessed=12 * rows * heads * HEAD, transcendentals=0
        ),
        name="unpack",
    )(grads)


def swap(x, axis):
    return lax.all_to_all(x, axis, split_axis=0, concat_axis=0, tiled=True)


def shards(
    features,
    query_states,
    key_states,
    value_states,
    cotangent,
    adapter_down,
    adapter_up,
    block_lists,
    block_counts,
):
    zones = lax.axis_size("zone")
    windows = lax.axis_size("dp")
    rows = query_states.shape[1]
    rank = adapter_down.shape[1]
    all_rows = zones * rows
    blocks = all_rows // BLK
    own_blocks = rows // BLK
    nbr = block_lists.shape[2]
    x = features[0]

    meta = jnp.concatenate([block_lists[0], block_counts[0][:, None]], axis=1).astype(BF)
    meta = jnp.pad(meta, ((0, META - own_blocks), (0, HEAD - nbr - 1)))
    sent = pack(meta, query_states[0], key_states[0], value_states[0], cotangent[0])
    states = swap(sent, "zone")

    info = states[:, 4 * rows:4 * rows + own_blocks, :nbr + 1].astype(jnp.int32)
    info = info.reshape(blocks, nbr + 1)
    counts = info[:, nbr]
    own = jnp.arange(blocks, dtype=jnp.int32)[:, None]
    slot = jnp.arange(nbr, dtype=jnp.int32)[None, :]
    ids = jnp.concatenate([own, jnp.where(slot < counts[:, None], info[:, :nbr], own)], axis=1)

    low = dot(x, adapter_down.reshape(2 * rank, -1), NT).astype(BF)
    low = jnp.broadcast_to(low[None], (zones, rows, 2 * rank))
    low, states = lax.optimization_barrier((low, states))
    low_all = swap(low, "zone")

    grads = attention(ids, counts, states, rows)
    grads, low_all = lax.optimization_barrier((grads, low_all))
    home = swap(grads, "zone")

    stacked = grads.reshape(zones, 3, rows, HEAD)
    up = jnp.stack(
        [
            jnp.einsum(
                "zra,zrf->af",
                low_all[:, :, t * rank:(t + 1) * rank],
                stacked[:, 1 + t],
                preferred_element_type=F32,
            )
            for t in range(2)
        ]
    )
    up = lax.psum(up, "dp")

    terms = down_terms(home, adapter_up, x)
    terms = swap(terms, "zone")
    query_grad, key_grad, value_grad = unpack(home)
    down = jnp.sum(terms.astype(F32), axis=0)
    down = swap(jnp.broadcast_to(down.astype(BF)[None], (windows,) + down.shape), "dp")
    factor = 1.0 / math.sqrt(windows * all_rows)
    down = jnp.sum(down.astype(F32), axis=0).reshape(2, rank, HEAD) * factor
    return (query_grad[None], key_grad[None], value_grad[None], down, up * factor)


def solution(mesh):
    rows = P("dp", "zone", None)
    cols = P(None, None, "zone")
    in_specs = (rows, rows, rows, rows, rows, P(), P(), rows, P("dp", "zone"))
    out_specs = (rows, rows, rows, cols, cols)
    return jax.shard_map(shards, mesh=mesh, in_specs=in_specs, out_specs=out_specs, check_vma=False)
```

```python
import functools
import math

import jax
import jax.numpy as jnp
from jax import lax
from jax.experimental import pallas as pl
from jax.experimental.pallas import tpu as pltpu
from jax.sharding import PartitionSpec as P

HEAD = 128
BLK = 64
VMEM_ALL = 60 << 20
TILE = 16
META = 16
BF = jnp.bfloat16
F32 = jnp.float32
NT = (((1,), (1,)), ((), ()))
TN = (((0,), (0,)), ((), ()))
NN = (((1,), (0,)), ((), ()))


def dot(a, b, dims):
    return lax.dot_general(a, b, dims, preferred_element_type=F32)


def whole(shape, space=pltpu.VMEM):
    return pl.BlockSpec(memory_space=space)


def pack_kernel(lists_ref, counts_ref, q_ref, k_ref, v_ref, g_ref, out_ref):
    rows = q_ref.shape[0]
    blocks, nbr = lists_ref.shape
    row = lax.broadcasted_iota(jnp.int32, (META, HEAD), 0)
    lane = lax.broadcasted_iota(jnp.int32, (META, HEAD), 1)
    meta = jnp.zeros((META, HEAD), jnp.int32)
    for b in range(blocks):
        for n in range(nbr + 1):
            value = counts_ref[0, b] if n == nbr else lists_ref[b, n]
            meta = jnp.where((row == b) & (lane == n), value, meta)
    meta = meta.astype(F32).astype(BF)
    for j in range(out_ref.shape[0]):
        cols = slice(j * HEAD, (j + 1) * HEAD)
        for t, ref in enumerate((q_ref, k_ref, v_ref, g_ref)):
            out_ref[j, t * rows:(t + 1) * rows, :] = ref[:, cols]
        out_ref[j, 4 * rows:, :] = meta


def pack(lists, counts, q, k, v, g, heads_per_step=16):
    rows, feats = q.shape
    heads = feats // HEAD
    out_rows = 4 * rows + META
    spec = pl.BlockSpec((rows, heads_per_step * HEAD), lambda i: (0, i))
    return pl.pallas_call(
        pack_kernel,
        grid=(heads // heads_per_step,),
        in_specs=[pl.BlockSpec(memory_space=pltpu.SMEM)] * 2 + [spec] * 4,
        out_specs=pl.BlockSpec((heads_per_step, out_rows, HEAD), lambda i: (i, 0, 0)),
        out_shape=jax.ShapeDtypeStruct((heads, out_rows, HEAD), BF),
        compiler_params=pltpu.CompilerParams(vmem_limit_bytes=VMEM_ALL),
        cost_estimate=pl.CostEstimate(flops=0, bytes_accessed=16 * rows * feats, transcendentals=0),
        name="pack",
    )(lists, counts, q, k, v, g)


def lowrank_kernel(x_ref, down_ref, out_ref):
    low = dot(x_ref[...], down_ref[...], NT).astype(BF)
    for j in range(out_ref.shape[0]):
        out_ref[j] = low


def lowrank(x, down, copies):
    rows, feats = x.shape
    return pl.pallas_call(
        lowrank_kernel,
        in_specs=[pl.BlockSpec(memory_space=pltpu.VMEM)] * 2,
        out_specs=pl.BlockSpec(memory_space=pltpu.VMEM),
        out_shape=jax.ShapeDtypeStruct((copies, rows, down.shape[0]), BF),
        compiler_params=pltpu.CompilerParams(vmem_limit_bytes=VMEM_ALL),
        cost_estimate=pl.CostEstimate(
            flops=2 * rows * feats * down.shape[0], bytes_accessed=6 * rows * feats, transcendentals=0
        ),
        name="lowrank",
    )(x, down)


def blockdiag(x):
    zero = jnp.zeros((BLK, HEAD), BF)
    upper = jnp.concatenate([x[:BLK], zero], axis=1)
    lower = jnp.concatenate([zero, x[BLK:]], axis=1)
    return jnp.concatenate([upper, lower], axis=0)


def attention_kernel(ids_ref, counts_ref, states_ref, out_ref, dq_ref, dk_ref, dv_ref, *scratch, rows, slots):
    pairs = out_ref.shape[0]
    scale = HEAD ** (-0.5)
    part_tiles, block_tiles = rows // TILE, BLK // TILE
    stride = 4 * part_tiles + META // TILE
    to_exp2 = scale * math.log2(math.e)
    s_bufs, g_bufs, w_bufs, d_bufs = (scratch[2 * i:2 * i + 2] for i in range(4))
    first_half = lax.broadcasted_iota(jnp.int32, (1, 2 * BLK), 1) < BLK

    def load(first, tiles):
        return states_ref[pl.ds(first, tiles)].reshape(tiles * TILE, HEAD)

    def of_slot(p, s):
        return [ids_ref[(2 * p + c) * slots + s] for c in range(2)]

    def own(p, part):
        return blockdiag(load(p * stride + part * part_tiles, part_tiles))

    def gathered(p, part):
        tiles = []
        for s in range(slots):
            at = [(code & 0xFFFF) + part * part_tiles for code in of_slot(p, s)]
            tiles.append(jnp.concatenate([load(a, block_tiles) for a in at], axis=1))
        return jnp.concatenate(tiles, axis=0)

    def products(p, s_buf, g_buf):
        s_buf[...] = dot(gathered(p, 1), own(p, 0), NT)
        g_buf[...] = dot(gathered(p, 2), own(p, 3), NT)

    def softmax(p, s_buf, g_buf, w_buf, d_buf):
        count = jnp.where(first_half, counts_ref[2 * p], counts_ref[2 * p + 1])
        tiles = [slice(s * BLK, (s + 1) * BLK) for s in range(slots)]
        fold = lambda op, x: functools.reduce(op, [x[r:r + 8] for r in range(0, BLK, 8)])
        top = None
        for s, at in enumerate(tiles):
            part = fold(jnp.maximum, s_buf[at, :])
            part = jnp.where(s <= count, part, -jnp.inf)
            top = part if top is None else jnp.maximum(top, part)
        top = jnp.max(top, axis=0, keepdims=True)
        total = None
        for s, at in enumerate(tiles):
            expd = jnp.exp2((s_buf[at, :] - jnp.where(s <= count, top, jnp.inf)) * to_exp2)
            s_buf[at, :] = expd
            part = fold(jnp.add, expd)
            total = part if total is None else total + part
        inverse = 1.0 / jnp.sum(total, axis=0, keepdims=True)
        delta = None
        for at in tiles:
            weights_b = (s_buf[at, :] * inverse).astype(BF)
            w_buf[at, :] = weights_b
            part = fold(jnp.add, weights_b.astype(F32) * g_buf[at, :])
            delta = part if delta is None else delta + part
        delta = jnp.sum(delta, axis=0, keepdims=True)
        for at in tiles:
            d_buf[at, :] = (s_buf[at, :] * inverse * (g_buf[at, :] - delta)).astype(BF)

    def gradients(p, w_buf, d_buf):
        q_bd = own(p, 0)
        g_bd = own(p, 3)
        dk = dot(d_buf[...], q_bd, NN)
        dv = dot(w_buf[...], g_bd, NN)
        for s in range(slots):
            for c, code in enumerate(of_slot(p, s)):
                at = code >> 16
                part = (slice(s * BLK, (s + 1) * BLK), slice(c * HEAD, (c + 1) * HEAD))
                dk_ref[at] += dk[part]
                dv_ref[at] += dv[part]
        dq = dot(d_buf[...], gathered(p, 1), TN)
        dq_ref[p, :BLK, :] = (dq[:BLK, :HEAD] * scale).astype(BF)
        dq_ref[p, BLK:, :] = (dq[BLK:, HEAD:] * scale).astype(BF)

    def step(p, c, a=True, b=True, g=True):
        if g:
            gradients(p - 2, w_bufs[c], d_bufs[c])
        if a:
            products(p, s_bufs[c], g_bufs[c])
        if b:
            softmax(p - 1, s_bufs[1 - c], g_bufs[1 - c], w_bufs[1 - c], d_bufs[1 - c])

    dk_ref[...] = jnp.zeros_like(dk_ref)
    dv_ref[...] = jnp.zeros_like(dv_ref)
    step(0, 0, b=False, g=False)
    step(1, 1, g=False)

    def body(i, carry):
        step(2 * i, 0)
        step(2 * i + 1, 1)
        return carry

    lax.fori_loop(1, pairs // 2, body, 0)
    step(pairs, 0, a=False)
    step(pairs + 1, 1, a=False, b=False)

    def finish(p, carry):
        at = pl.ds(2 * p, 2)
        out_ref[p, :rows, :] = (dk_ref[at].reshape(rows, HEAD) * scale).astype(BF)
        out_ref[p, rows:, :] = dv_ref[at].reshape(rows, HEAD).astype(BF)
        return carry

    lax.fori_loop(0, pairs, finish, 0)


def attention(ids, counts, states, rows):
    pairs = states.shape[0]
    slots = ids.shape[1]
    all_rows = pairs * rows
    stride = states.shape[1] // TILE
    ids = (ids >> 1) * stride + (ids & 1) * (BLK // TILE) | (ids << 16)
    wide = (slots * BLK, 2 * BLK)
    return pl.pallas_call(
        functools.partial(attention_kernel, rows=rows, slots=slots),
        in_specs=[
            pl.BlockSpec(memory_space=pltpu.SMEM),
            pl.BlockSpec(memory_space=pltpu.SMEM),
            pl.BlockSpec(memory_space=pltpu.VMEM),
        ],
        out_specs=[pl.BlockSpec(memory_space=pltpu.VMEM)] * 2,
        out_shape=[
            jax.ShapeDtypeStruct((pairs, 2 * rows, HEAD), BF),
            jax.ShapeDtypeStruct((pairs, rows, HEAD), BF),
        ],
        scratch_shapes=[pltpu.VMEM((all_rows // BLK, BLK, HEAD), F32)] * 2
        + [pltpu.VMEM(wide, F32)] * 4
        + [pltpu.VMEM(wide, BF)] * 4,
        compiler_params=pltpu.CompilerParams(vmem_limit_bytes=VMEM_ALL),
        cost_estimate=pl.CostEstimate(
            flops=2 * 5 * all_rows * slots * BLK * HEAD * 2,
            bytes_accessed=states.size * 2 + pairs * 3 * rows * HEAD * 2,
            transcendentals=all_rows * slots * BLK,
        ),
        name="attention",
    )(ids.reshape(-1), counts, states.reshape(-1, TILE, HEAD))


def down_kernel(grads_ref, up_ref, x_ref, out_ref):
    heads = grads_ref.shape[0]
    rows, feats = x_ref.shape
    low = []
    for t in range(2):
        total = jnp.zeros((rows, up_ref.shape[1]), F32)
        for h in range(heads):
            part = grads_ref[h, t * rows:(t + 1) * rows, :]
            total += dot(part, up_ref[t, :, h * HEAD:(h + 1) * HEAD], NT)
        low.append(total)
    back_low = jnp.concatenate(low, axis=1).astype(BF)
    for h in range(heads):
        out_ref[h] = dot(back_low, x_ref[:, h * HEAD:(h + 1) * HEAD], TN).astype(BF)


def down_terms(grads, adapter_up, x):
    heads = grads.shape[0]
    rows, feats = x.shape
    return pl.pallas_call(
        down_kernel,
        in_specs=[pl.BlockSpec(memory_space=pltpu.VMEM)] * 3,
        out_specs=pl.BlockSpec(memory_space=pltpu.VMEM),
        out_shape=jax.ShapeDtypeStruct((heads, 2 * adapter_up.shape[1], HEAD), BF),
        compiler_params=pltpu.CompilerParams(vmem_limit_bytes=VMEM_ALL),
        cost_estimate=pl.CostEstimate(
            flops=8 * rows * feats * adapter_up.shape[1],
            bytes_accessed=12 * rows * feats,
            transcendentals=0,
        ),
        name="down_terms",
    )(grads, adapter_up, x)


def unpack(grads, rows):
    parts = grads.reshape(grads.shape[0], -1, rows, HEAD)
    return [parts[:, t].transpose(1, 0, 2).reshape(rows, -1) for t in range(parts.shape[1])]


def swap(x, axis):
    return lax.all_to_all(x, axis, split_axis=0, concat_axis=0, tiled=True)


def sum_windows(x):
    n = lax.axis_size("dp")
    step = 1
    while step < n:
        x = x + lax.ppermute(x, "dp", [(i, i ^ step) for i in range(n)])
        step *= 2
    return x


def shards(
    features,
    query_states,
    key_states,
    value_states,
    cotangent,
    adapter_down,
    adapter_up,
    block_lists,
    block_counts,
):
    zones = lax.axis_size("zone")
    windows = lax.axis_size("dp")
    rows = query_states.shape[1]
    rank = adapter_down.shape[1]
    all_rows = zones * rows
    blocks = all_rows // BLK
    own_blocks = rows // BLK
    nbr = block_lists.shape[2]
    x = features[0]

    sent = pack(
        block_lists[0], block_counts, query_states[0], key_states[0], value_states[0], cotangent[0]
    )
    states = swap(sent, "zone")

    info = states[:, 4 * rows:4 * rows + own_blocks, :nbr + 1].astype(jnp.int32)
    info = info.reshape(blocks, nbr + 1)
    counts = info[:, nbr]
    own = jnp.arange(blocks, dtype=jnp.int32)[:, None]
    slot = jnp.arange(nbr, dtype=jnp.int32)[None, :]
    ids = jnp.concatenate([own, jnp.where(slot < counts[:, None], info[:, :nbr], own)], axis=1)

    low = lowrank(x, adapter_down.reshape(2 * rank, -1), zones)
    low, states = lax.optimization_barrier((low, states))
    low_all = swap(low, "zone")

    grads, dq = attention(ids, counts, states, rows)
    grads, low_all = lax.optimization_barrier((grads, low_all))
    home = swap(grads, "zone")

    stacked = grads.reshape(zones, 2, rows, HEAD)
    up = jnp.concatenate(
        [
            jnp.einsum(
                "zra,zrf->af",
                low_all[:, :, t * rank:(t + 1) * rank],
                stacked[:, t],
                preferred_element_type=F32,
            )
            for t in range(2)
        ]
    )
    up = sum_windows(up)

    terms, up = lax.optimization_barrier((down_terms(home, adapter_up, x), up))
    terms = swap(terms, "zone")
    key_grad, value_grad = unpack(home, rows)
    dq, terms, key_grad, value_grad = lax.optimization_barrier((dq, terms, key_grad, value_grad))
    dq = swap(dq, "zone")
    down = sum_windows(jnp.sum(terms.astype(F32), axis=0))
    (query_grad,) = unpack(dq, rows)
    factor = 1.0 / math.sqrt(windows * all_rows)
    return (
        query_grad[None],
        key_grad[None],
        value_grad[None],
        down.reshape(2, rank, HEAD) * factor,
        up.reshape(2, rank, HEAD) * factor,
    )


def solution(mesh):
    rows = P("dp", "zone", None)
    cols = P(None, None, "zone")
    in_specs = (rows, rows, rows, rows, rows, P(), P(), rows, P("dp", "zone"))
    out_specs = (rows, rows, rows, cols, cols)
    return jax.shard_map(shards, mesh=mesh, in_specs=in_specs, out_specs=out_specs, check_vma=False)
```

```python
import functools
import math

import jax
import jax.numpy as jnp
from jax import lax
from jax.experimental import pallas as pl
from jax.experimental.pallas import tpu as pltpu
from jax.sharding import PartitionSpec as P

HEAD = 128
BLK = 64
VMEM_ALL = 63 << 20
TILE = 16
LIST = 16
META = 16
BF = jnp.bfloat16
F32 = jnp.float32
NT = (((1,), (1,)), ((), ()))
TN = (((0,), (0,)), ((), ()))
NN = (((1,), (0,)), ((), ()))


def dot(a, b, dims):
    return lax.dot_general(a, b, dims, preferred_element_type=F32)


def whole(shape, space=pltpu.VMEM):
    return pl.BlockSpec(memory_space=space)


def pack_kernel(lists_ref, counts_ref, q_ref, k_ref, v_ref, g_ref, out_ref):
    rows = q_ref.shape[0]
    blocks, nbr = lists_ref.shape
    row = lax.broadcasted_iota(jnp.int32, (META, HEAD), 0)
    lane = lax.broadcasted_iota(jnp.int32, (META, HEAD), 1)
    meta = jnp.zeros((META, HEAD), jnp.int32)
    for b in range(blocks):
        for n in range(nbr + 1):
            value = lists_ref[b, n - 1] if n else counts_ref[0, b]
            meta = jnp.where((row == 0) & (lane == b * LIST + n), value, meta)
    meta = meta.astype(F32).astype(BF)
    for j in range(out_ref.shape[0]):
        cols = slice(j * HEAD, (j + 1) * HEAD)
        for t, ref in enumerate((q_ref, k_ref, v_ref, g_ref)):
            out_ref[j, t * rows:(t + 1) * rows, :] = ref[:, cols]
        out_ref[j, 4 * rows:, :] = meta


def pack(lists, counts, q, k, v, g, heads_per_step=16):
    rows, feats = q.shape
    heads = feats // HEAD
    out_rows = 4 * rows + META
    spec = pl.BlockSpec((rows, heads_per_step * HEAD), lambda i: (0, i))
    return pl.pallas_call(
        pack_kernel,
        grid=(heads // heads_per_step,),
        in_specs=[pl.BlockSpec(memory_space=pltpu.SMEM)] * 2 + [spec] * 4,
        out_specs=pl.BlockSpec((heads_per_step, out_rows, HEAD), lambda i: (i, 0, 0)),
        out_shape=jax.ShapeDtypeStruct((heads, out_rows, HEAD), BF),
        compiler_params=pltpu.CompilerParams(vmem_limit_bytes=VMEM_ALL),
        cost_estimate=pl.CostEstimate(flops=0, bytes_accessed=16 * rows * feats, transcendentals=0),
        name="pack",
    )(lists, counts, q, k, v, g)


def lowrank_kernel(x_ref, down_ref, out_ref):
    low = dot(x_ref[...], down_ref[...], NT).astype(BF)
    for j in range(out_ref.shape[0]):
        out_ref[j] = low


def lowrank(x, down, copies):
    rows, feats = x.shape
    return pl.pallas_call(
        lowrank_kernel,
        in_specs=[pl.BlockSpec(memory_space=pltpu.VMEM)] * 2,
        out_specs=pl.BlockSpec(memory_space=pltpu.VMEM),
        out_shape=jax.ShapeDtypeStruct((copies, rows, down.shape[0]), BF),
        compiler_params=pltpu.CompilerParams(vmem_limit_bytes=VMEM_ALL),
        cost_estimate=pl.CostEstimate(
            flops=2 * rows * feats * down.shape[0], bytes_accessed=6 * rows * feats, transcendentals=0
        ),
        name="lowrank",
    )(x, down)


def blockdiag(x):
    zero = jnp.zeros((BLK, HEAD), BF)
    upper = jnp.concatenate([x[:BLK], zero], axis=1)
    lower = jnp.concatenate([zero, x[BLK:]], axis=1)
    return jnp.concatenate([upper, lower], axis=0)


def attention_kernel(
    states_hbm,
    out_hbm,
    dq_hbm,
    states_ref,
    out_ref,
    dq_ref,
    dk_ref,
    dv_ref,
    meta_ref,
    codes_ref,
    ids_ref,
    offset_ref,
    order_ref,
    sems,
    *scratch,
    slots,
):
    blocks = dk_ref.shape[0]
    pairs = blocks // 2
    stride = states_hbm.shape[1]
    block_tiles = BLK // TILE
    part_tiles = 2 * block_tiles
    least = 2
    scale = HEAD ** (-0.5)
    to_exp2 = scale * math.log2(math.e)
    s_bufs, g_bufs, w_bufs, d_bufs = (scratch[2 * i:2 * i + 2] for i in range(4))
    first_half = lax.broadcasted_iota(jnp.int32, (1, 2 * BLK), 1) < BLK

    copy_meta = pltpu.make_async_copy(states_hbm.at[:, stride - 1], meta_ref, sems.at[0])
    copy_meta.start()
    copy_states = pltpu.make_async_copy(states_hbm, states_ref, sems.at[1])
    copy_states.start()
    dk_ref[...] = jnp.zeros_like(dk_ref)
    dv_ref[...] = jnp.zeros_like(dv_ref)

    copy_meta.wait()
    info = jnp.sum(meta_ref[...].astype(F32), axis=1).astype(jnp.int32)
    lane = lax.broadcasted_iota(jnp.int32, info.shape, 1)
    row = lax.broadcasted_iota(jnp.int32, info.shape, 0)
    second = lane >= LIST
    counts = [info[:, c * LIST:c * LIST + 1] for c in range(2)]
    count = jnp.where(second, counts[1], counts[0])
    slot = lane & (LIST - 1)
    ids = jnp.where((slot >= 1) & (slot <= count), info, 2 * row + jnp.where(second, 1, 0))
    codes = (ids >> 1) * stride + (ids & 1) * block_tiles | (ids << 16)
    for c in range(2):
        codes = jnp.where(lane == 2 * LIST + c, counts[c], codes)
    codes_ref[...] = codes
    copy_codes = pltpu.make_async_copy(codes_ref, ids_ref, sems.at[2])
    copy_codes.start()
    copy_codes.wait()

    def count_of(b):
        return ids_ref[b // 2, 2 * LIST + b % 2]

    for c in range(slots + 1):
        offset_ref[c] = 0
    for b in range(blocks):
        n = count_of(b)
        offset_ref[n] = offset_ref[n] + 1
    above = [None] * (slots + 1)
    total = 0
    for c in range(slots - 1, least - 1, -1):
        above[c] = total
        total = total + offset_ref[c]
        offset_ref[c] = above[c]
    for b in range(blocks):
        n = count_of(b)
        place = offset_ref[n]
        offset_ref[n] = place + 1
        order_ref[place] = b
    copy_states.wait()

    flat_ref = states_ref.reshape(pairs * stride, TILE, HEAD)

    def load(first, tiles):
        return flat_ref[pl.ds(first, tiles)].reshape(tiles * TILE, HEAD)

    def place_of(p):
        return [(b >> 1, b & 1) for b in (order_ref[2 * p + c] for c in range(2))]

    def of_slot(at, s):
        return [ids_ref[d, c * LIST + s] for d, c in at]

    def own(at, part):
        tiles = [load(d * stride + c * block_tiles + part * part_tiles, block_tiles) for d, c in at]
        return blockdiag(jnp.concatenate(tiles, axis=0))

    def gathered(at, part, n):
        tiles = []
        for s in range(n):
            first = [(code & 0xFFFF) + part * part_tiles for code in of_slot(at, s)]
            tiles.append(jnp.concatenate([load(f, block_tiles) for f in first], axis=1))
        return jnp.concatenate(tiles, axis=0)

    def products(p, n, s_buf, g_buf):
        at = place_of(p)
        s_buf[:n * BLK, :] = dot(gathered(at, 1, n), own(at, 0), NT)
        g_buf[:n * BLK, :] = dot(gathered(at, 2, n), own(at, 3), NT)

    def softmax(p, n, s_buf, g_buf, w_buf, d_buf):
        used = [ids_ref[d, 2 * LIST + c] for d, c in place_of(p)]
        count = jnp.where(first_half, used[0], used[1])
        tiles = [slice(s * BLK, (s + 1) * BLK) for s in range(n)]

        def fold(op, x):
            return functools.reduce(op, [x[r:r + 8] for r in range(0, BLK, 8)])

        top = None
        for s, at in enumerate(tiles):
            part = fold(jnp.maximum, s_buf[at, :])
            part = part if s <= least else jnp.where(s <= count, part, -jnp.inf)
            top = part if top is None else jnp.maximum(top, part)
        top = jnp.max(top, axis=0, keepdims=True)
        total = None
        for s, at in enumerate(tiles):
            shift = top if s <= least else jnp.where(s <= count, top, jnp.inf)
            expd = jnp.exp2((s_buf[at, :] - shift) * to_exp2)
            s_buf[at, :] = expd
            part = fold(jnp.add, expd)
            total = part if total is None else total + part
        inverse = 1.0 / jnp.sum(total, axis=0, keepdims=True)
        delta = None
        for at in tiles:
            weights_b = (s_buf[at, :] * inverse).astype(BF)
            w_buf[at, :] = weights_b
            part = fold(jnp.add, weights_b.astype(F32) * g_buf[at, :])
            delta = part if delta is None else delta + part
        delta = jnp.sum(delta, axis=0, keepdims=True)
        for at in tiles:
            d_buf[at, :] = (s_buf[at, :] * inverse * (g_buf[at, :] - delta)).astype(BF)

    def gradients(p, n, w_buf, d_buf):
        at = place_of(p)
        grad_scores = d_buf[:n * BLK, :]
        dk = dot(grad_scores, own(at, 0), NN)
        dv = dot(w_buf[:n * BLK, :], own(at, 3), NN)
        for s in range(n):
            for c, code in enumerate(of_slot(at, s)):
                block = code >> 16
                part = (slice(s * BLK, (s + 1) * BLK), slice(c * HEAD, (c + 1) * HEAD))
                dk_ref[block] += dk[part]
                dv_ref[block] += dv[part]
        dq = dot(grad_scores, gathered(at, 1, n), TN)
        for c, (d, half) in enumerate(at):
            part = dq[c * BLK:(c + 1) * BLK, c * HEAD:(c + 1) * HEAD]
            dq_ref[2 * d + half] = (part * scale).astype(BF)

    def step(p, c, n):
        gradients(p - 2, n, w_bufs[c], d_bufs[c])
        products(jnp.minimum(p, pairs - 1), n, s_bufs[c], g_bufs[c])
        softmax(
            jnp.minimum(p - 1, pairs - 1), n, s_bufs[1 - c], g_bufs[1 - c], w_bufs[1 - c], d_bufs[1 - c]
        )

    products(0, slots, s_bufs[0], g_bufs[0])
    products(1, slots, s_bufs[1], g_bufs[1])
    softmax(0, slots, s_bufs[0], g_bufs[0], w_bufs[0], d_bufs[0])
    first, last = 1, pairs // 2 + 1
    for n in range(slots, least, -1):

        def body(i, carry, n=n):
            step(2 * i, 0, n)
            step(2 * i + 1, 1, n)
            return carry

        until = last
        if n > least + 1:
            until = jnp.minimum(1 + ((above[n - 2] + 3) >> 2), last)
        lax.fori_loop(first, until, body, 0)
        first = until

    copy_dq = pltpu.make_async_copy(dq_ref, dq_hbm, sems.at[3])
    copy_dq.start()
    chunk = blocks // 4
    copies = []
    for start in range(0, blocks, chunk):

        def finish(b, carry):
            half = pl.ds(pl.multiple_of((b & 1) * BLK, BLK), BLK)
            out_ref[b >> 1, 0, half, :] = (dk_ref[b] * scale).astype(BF)
            out_ref[b >> 1, 1, half, :] = dv_ref[b].astype(BF)
            return carry

        lax.fori_loop(start, start + chunk, finish, 0, unroll=4)
        at = pl.ds(start // 2, chunk // 2)
        copies.append(
            pltpu.make_async_copy(out_ref.at[at], out_hbm.at[at], sems.at[4 + start // chunk])
        )
        copies[-1].start()
    copy_dq.wait()
    for copy in copies:
        copy.wait()


def attention(states, rows, slots):
    pairs = states.shape[0]
    blocks = pairs * rows // BLK
    tiles = states.shape[1] // TILE
    wide = (slots * BLK, 2 * BLK)
    out_shape = [
        jax.ShapeDtypeStruct((pairs, 2, rows, HEAD), BF),
        jax.ShapeDtypeStruct((blocks, BLK, HEAD), BF),
    ]
    grads, dq = pl.pallas_call(
        functools.partial(attention_kernel, slots=slots),
        in_specs=[pl.BlockSpec(memory_space=pl.ANY)],
        out_specs=[pl.BlockSpec(memory_space=pl.ANY)] * 2,
        out_shape=out_shape,
        scratch_shapes=[pltpu.VMEM((pairs, tiles, TILE, HEAD), BF)]
        + [pltpu.VMEM(out.shape, BF) for out in out_shape]
        + [pltpu.VMEM((blocks, BLK, HEAD), F32)] * 2
        + [
            pltpu.VMEM((pairs, META, HEAD), BF),
            pltpu.VMEM((pairs, HEAD), jnp.int32),
            pltpu.SMEM((pairs, HEAD), jnp.int32),
            pltpu.SMEM((LIST,), jnp.int32),
            pltpu.SMEM((blocks,), jnp.int32),
            pltpu.SemaphoreType.DMA((8,)),
        ]
        + [pltpu.VMEM(wide, F32)] * 4
        + [pltpu.VMEM(wide, BF)] * 4,
        compiler_params=pltpu.CompilerParams(vmem_limit_bytes=VMEM_ALL),
        cost_estimate=pl.CostEstimate(
            flops=20 * blocks * slots * BLK * BLK * HEAD,
            bytes_accessed=2 * states.size + 6 * blocks * BLK * HEAD,
            transcendentals=blocks * slots * BLK * BLK,
        ),
        name="attention",
    )(states.reshape(pairs, tiles, TILE, HEAD))
    return grads.reshape(pairs, 2 * rows, HEAD), dq.reshape(pairs, rows, HEAD)


def down_kernel(grads_ref, up_ref, x_ref, out_ref):
    heads = grads_ref.shape[0]
    rows = x_ref.shape[0]
    low = []
    for t in range(2):
        part = slice(t * rows, (t + 1) * rows)
        full = jnp.concatenate([grads_ref[h, part, :] for h in range(heads)], axis=1)
        low.append(dot(full, up_ref[t], NT))
    back_low = jnp.concatenate(low, axis=1).astype(BF)
    terms = dot(back_low, x_ref[...], TN).astype(BF)
    for h in range(heads):
        out_ref[h] = terms[:, h * HEAD:(h + 1) * HEAD]


def down_terms(grads, adapter_up, x):
    heads = grads.shape[0]
    rows, feats = x.shape
    return pl.pallas_call(
        down_kernel,
        in_specs=[pl.BlockSpec(memory_space=pltpu.VMEM)] * 3,
        out_specs=pl.BlockSpec(memory_space=pltpu.VMEM),
        out_shape=jax.ShapeDtypeStruct((heads, 2 * adapter_up.shape[1], HEAD), BF),
        compiler_params=pltpu.CompilerParams(vmem_limit_bytes=VMEM_ALL),
        cost_estimate=pl.CostEstimate(
            flops=8 * rows * feats * adapter_up.shape[1],
            bytes_accessed=12 * rows * feats,
            transcendentals=0,
        ),
        name="down_terms",
    )(grads, adapter_up, x)


def unpack(grads, rows):
    parts = grads.reshape(grads.shape[0], -1, rows, HEAD)
    return [parts[:, t].transpose(1, 0, 2).reshape(rows, -1) for t in range(parts.shape[1])]


def swap(x, axis):
    return lax.all_to_all(x, axis, split_axis=0, concat_axis=0, tiled=True)


def sum_windows(x):
    n = lax.axis_size("dp")
    if n % 8 or n > 8:
        step = 1
        while step < n:
            x = x + lax.ppermute(x, "dp", [(i, i ^ step) for i in range(n)])
            step *= 2
        return x
    near = [lax.ppermute(x, "dp", [(i, i ^ step) for i in range(n)]) for step in (1, 2, 3)]
    x = (x + near[0]) + (near[1] + near[2])
    return x + lax.ppermute(x, "dp", [(i, (i + (2 if i % 4 >= 2 else -2)) % n) for i in range(n)])


def shards(
    features,
    query_states,
    key_states,
    value_states,
    cotangent,
    adapter_down,
    adapter_up,
    block_lists,
    block_counts,
):
    zones = lax.axis_size("zone")
    windows = lax.axis_size("dp")
    rows = query_states.shape[1]
    rank = adapter_down.shape[1]
    all_rows = zones * rows
    x = features[0]

    sent = pack(
        block_lists[0], block_counts, query_states[0], key_states[0], value_states[0], cotangent[0]
    )
    states = swap(sent, "zone")

    low = lowrank(x, adapter_down.reshape(2 * rank, -1), zones)
    low, states = lax.optimization_barrier((low, states))
    low_all = swap(low, "zone")

    grads, dq = attention(states, rows, block_lists.shape[2] + 1)
    grads, low_all = lax.optimization_barrier((grads, low_all))
    home = swap(grads, "zone")

    stacked = grads.reshape(zones, 2, rows, HEAD)
    up = jnp.concatenate(
        [
            jnp.einsum(
                "zra,zrf->af",
                low_all[:, :, t * rank:(t + 1) * rank],
                stacked[:, t],
                preferred_element_type=F32,
            )
            for t in range(2)
        ]
    )
    up = sum_windows(up)

    terms, up = lax.optimization_barrier((down_terms(home, adapter_up, x), up))
    terms = swap(terms, "zone")
    key_grad, value_grad = unpack(home, rows)
    dq, terms, key_grad, value_grad = lax.optimization_barrier((dq, terms, key_grad, value_grad))
    dq = swap(dq, "zone")
    down = sum_windows(jnp.sum(terms.astype(F32), axis=0))
    (query_grad,) = unpack(dq, rows)
    factor = 1.0 / math.sqrt(windows * all_rows)
    return (
        query_grad[None],
        key_grad[None],
        value_grad[None],
        down.reshape(2, rank, HEAD) * factor,
        up.reshape(2, rank, HEAD) * factor,
    )


def solution(mesh):
    rows = P("dp", "zone", None)
    cols = P(None, None, "zone")
    in_specs = (rows, rows, rows, rows, rows, P(), P(), rows, P("dp", "zone"))
    out_specs = (rows, rows, rows, cols, cols)
    return jax.shard_map(shards, mesh=mesh, in_specs=in_specs, out_specs=out_specs, check_vma=False)
```

```python
import functools
import math

import jax
import jax.numpy as jnp
from jax import lax
from jax.experimental import pallas as pl
from jax.experimental.pallas import tpu as pltpu
from jax.sharding import PartitionSpec as P

HEAD = 128
BLK = 64
VMEM_ALL = 63 << 20
VMEM_SOME = 12 << 20
TILE = 16
LIST = 16
META = 16
CHUNKS = 4
PACK_CHUNKS = 2
BF = jnp.bfloat16
F32 = jnp.float32
NT = (((1,), (1,)), ((), ()))
TN = (((0,), (0,)), ((), ()))
NN = (((1,), (0,)), ((), ()))


def dot(a, b, dims):
    return lax.dot_general(a, b, dims, preferred_element_type=F32)


def whole(shape, space=pltpu.VMEM):
    return pl.BlockSpec(memory_space=space)


def pack_kernel(lists_ref, counts_ref, *refs):
    ins, (x_hbm, down_hbm, out_hbm), refs = refs[:4], refs[4:7], refs[7:]
    bufs, (x_ref, down_ref, out_ref, sems) = refs[:4], refs[4:]
    rows, feats = bufs[0].shape
    heads = feats // HEAD
    chunk = feats // PACK_CHUNKS
    states_rows = 4 * rows + META
    reads = []
    for i in range(PACK_CHUNKS):
        at = (slice(None), pl.ds(i * chunk, chunk))
        for t in range(4):
            reads.append(
                pltpu.make_async_copy(ins[t].at[at], bufs[t].at[at], sems.at[i * 4 + t])
            )
            reads[-1].start()
    last = 5 * PACK_CHUNKS
    others = [
        pltpu.make_async_copy(x_hbm, x_ref, sems.at[last]),
        pltpu.make_async_copy(down_hbm, down_ref, sems.at[last + 1]),
    ]
    for read in others:
        read.start()
    blocks, nbr = lists_ref.shape
    row = lax.broadcasted_iota(jnp.int32, (META, HEAD), 0)
    lane = lax.broadcasted_iota(jnp.int32, (META, HEAD), 1)
    meta = jnp.zeros((META, HEAD), jnp.int32)
    for b in range(blocks):
        for n in range(nbr + 1):
            value = lists_ref[b, n - 1] if n else counts_ref[0, b]
            meta = jnp.where((row == 0) & (lane == b * LIST + n), value, meta)
    meta = meta.astype(F32).astype(BF)
    writes = []
    for i in range(PACK_CHUNKS):
        for t in range(4):
            reads[i * 4 + t].wait()
        here = heads // PACK_CHUNKS
        for j in range(i * here, (i + 1) * here):
            cols = slice(j * HEAD, (j + 1) * HEAD)
            for t in range(4):
                out_ref[j, t * rows:(t + 1) * rows, :] = bufs[t][:, cols]
            out_ref[j, 4 * rows:states_rows, :] = meta
        at = (pl.ds(i * here, here), pl.ds(0, states_rows))
        writes.append(pltpu.make_async_copy(out_ref.at[at], out_hbm.at[at], sems.at[4 * PACK_CHUNKS + i]))
        writes[-1].start()
    for read in others:
        read.wait()
    low = dot(x_ref[...], down_ref[...], NT).astype(BF)
    half, rank = rows // 2, low.shape[1] // 2
    for t in range(2):
        part = low[:, t * rank:(t + 1) * rank]
        part = jnp.concatenate([part[:half], part[half:]], axis=1)
        for j in range(t, heads, 2):
            out_ref[j, states_rows:, :] = part
    at = (slice(None), pl.ds(states_rows, half))
    writes.append(pltpu.make_async_copy(out_ref.at[at], out_hbm.at[at], sems.at[last]))
    writes[-1].start()
    for write in writes:
        write.wait()


def pack(lists, counts, q, k, v, g, x, down):
    rows, feats = q.shape
    out = (feats // HEAD, 4 * rows + META + rows // 2, HEAD)
    return pl.pallas_call(
        pack_kernel,
        in_specs=[pl.BlockSpec(memory_space=pltpu.SMEM)] * 2
        + [pl.BlockSpec(memory_space=pl.ANY)] * 6,
        out_specs=pl.BlockSpec(memory_space=pl.ANY),
        out_shape=jax.ShapeDtypeStruct(out, BF),
        scratch_shapes=[pltpu.VMEM((rows, feats), BF)] * 5
        + [
            pltpu.VMEM(down.shape, BF),
            pltpu.VMEM(out, BF),
            pltpu.SemaphoreType.DMA((5 * PACK_CHUNKS + 2,)),
        ],
        compiler_params=pltpu.CompilerParams(vmem_limit_bytes=VMEM_ALL),
        cost_estimate=pl.CostEstimate(flops=0, bytes_accessed=16 * rows * feats, transcendentals=0),
        name="pack",
    )(lists, counts, q, k, v, g, x, down)


def up_kernel(parity_ref, own_ref, other_ref, grads_ref, out_ref):
    parts, half, lanes = own_ref.shape
    rank = lanes // 2
    mine, other = own_ref[...], other_ref[...]
    for t in range(2):
        low = jnp.where(parity_ref[0] == t, mine, other).reshape(parts * half, lanes)
        first = 2 * t * half
        grads = jnp.concatenate(
            [
                grads_ref[:, first:first + half, :].reshape(parts * half, HEAD),
                grads_ref[:, first + half:first + 2 * half, :].reshape(parts * half, HEAD),
            ],
            axis=1,
        )
        both = dot(low, grads, TN)
        out_ref[t * rank:(t + 1) * rank, :] = both[:rank, :HEAD] + both[rank:, HEAD:]


def up_terms(parity, own, other, grads):
    lanes = own.shape[2]
    return pl.pallas_call(
        up_kernel,
        in_specs=[pl.BlockSpec(memory_space=pltpu.SMEM)]
        + [pl.BlockSpec(memory_space=pltpu.VMEM)] * 3,
        out_specs=pl.BlockSpec(memory_space=pltpu.VMEM),
        out_shape=jax.ShapeDtypeStruct((lanes, HEAD), F32),
        compiler_params=pltpu.CompilerParams(vmem_limit_bytes=VMEM_SOME),
        cost_estimate=pl.CostEstimate(
            flops=4 * own.size * HEAD * 2, bytes_accessed=4 * own.size + 2 * grads.size, transcendentals=0
        ),
        name="up_terms",
    )(parity, own, other, grads)


def blockdiag(x):
    zero = jnp.zeros((BLK, HEAD), BF)
    upper = jnp.concatenate([x[:BLK], zero], axis=1)
    lower = jnp.concatenate([zero, x[BLK:]], axis=1)
    return jnp.concatenate([upper, lower], axis=0)


def attention_kernel(
    states_hbm,
    out_hbm,
    dq_hbm,
    states_ref,
    out_ref,
    dq_ref,
    dk_ref,
    dv_ref,
    meta_ref,
    codes_ref,
    ids_ref,
    offset_ref,
    order_ref,
    sems,
    *scratch,
    slots,
):
    blocks = dk_ref.shape[0]
    pairs = blocks // 2
    stride = states_ref.shape[1]
    block_tiles = BLK // TILE
    part_tiles = 2 * block_tiles
    least = 2
    scale = HEAD ** (-0.5)
    to_exp2 = scale * math.log2(math.e)
    s_bufs, g_bufs, w_bufs, d_bufs = (scratch[2 * i:2 * i + 2] for i in range(4))
    first_half = lax.broadcasted_iota(jnp.int32, (1, 2 * BLK), 1) < BLK

    copy_meta = pltpu.make_async_copy(states_hbm.at[:, stride - 1], meta_ref, sems.at[0])
    copy_meta.start()
    copy_states = pltpu.make_async_copy(states_hbm.at[:, pl.ds(0, stride)], states_ref, sems.at[1])
    copy_states.start()
    dk_ref[...] = jnp.zeros_like(dk_ref)

    copy_meta.wait()
    info = jnp.sum(meta_ref[...].astype(F32), axis=1).astype(jnp.int32)
    lane = lax.broadcasted_iota(jnp.int32, info.shape, 1)
    row = lax.broadcasted_iota(jnp.int32, info.shape, 0)
    second = lane >= LIST
    counts = [info[:, c * LIST:c * LIST + 1] for c in range(2)]
    count = jnp.where(second, counts[1], counts[0])
    slot = lane & (LIST - 1)
    ids = jnp.where((slot >= 1) & (slot <= count), info, 2 * row + jnp.where(second, 1, 0))
    codes = (ids >> 1) * stride + (ids & 1) * block_tiles | (ids << 16)
    for c in range(2):
        codes = jnp.where(lane == 2 * LIST + c, counts[c], codes)
    codes_ref[...] = codes
    copy_codes = pltpu.make_async_copy(codes_ref, ids_ref, sems.at[2])
    copy_codes.start()
    dv_ref[...] = jnp.zeros_like(dv_ref)
    copy_codes.wait()

    def count_of(b):
        return ids_ref[b // 2, 2 * LIST + b % 2]

    for c in range(slots + 1):
        offset_ref[c] = 0
    for b in range(blocks):
        n = count_of(b)
        offset_ref[n] = offset_ref[n] + 1
    above = [None] * (slots + 1)
    total = 0
    for c in range(slots - 1, least - 1, -1):
        above[c] = total
        total = total + offset_ref[c]
        offset_ref[c] = above[c]
    for b in range(blocks):
        n = count_of(b)
        place = offset_ref[n]
        offset_ref[n] = place + 1
        order_ref[place] = b
    copy_states.wait()

    flat_ref = states_ref.reshape(pairs * stride, TILE, HEAD)

    def load(first, tiles):
        return flat_ref[pl.ds(first, tiles)].reshape(tiles * TILE, HEAD)

    def place_of(p):
        return [(b >> 1, b & 1) for b in (order_ref[2 * p + c] for c in range(2))]

    def of_slot(at, s):
        return [ids_ref[d, c * LIST + s] for d, c in at]

    def own(at, part):
        tiles = [load(d * stride + c * block_tiles + part * part_tiles, block_tiles) for d, c in at]
        return blockdiag(jnp.concatenate(tiles, axis=0))

    def gathered(at, part, n):
        tiles = []
        for s in range(n):
            first = [(code & 0xFFFF) + part * part_tiles for code in of_slot(at, s)]
            tiles.append(jnp.concatenate([load(f, block_tiles) for f in first], axis=1))
        return jnp.concatenate(tiles, axis=0)

    def products(p, n, s_buf, g_buf):
        at = place_of(p)
        s_buf[:n * BLK, :] = dot(gathered(at, 1, n), own(at, 0), NT)
        g_buf[:n * BLK, :] = dot(gathered(at, 2, n), own(at, 3), NT)

    def softmax(p, n, s_buf, g_buf, w_buf, d_buf):
        used = [ids_ref[d, 2 * LIST + c] for d, c in place_of(p)]
        count = jnp.where(first_half, used[0], used[1])
        tiles = [slice(s * BLK, (s + 1) * BLK) for s in range(n)]

        def fold(op, x):
            return functools.reduce(op, [x[r:r + 8] for r in range(0, BLK, 8)])

        top = None
        for s, at in enumerate(tiles):
            part = fold(jnp.maximum, s_buf[at, :])
            part = part if s <= least else jnp.where(s <= count, part, -jnp.inf)
            top = part if top is None else jnp.maximum(top, part)
        top = jnp.max(top, axis=0, keepdims=True)
        total = None
        for s, at in enumerate(tiles):
            shift = top if s <= least else jnp.where(s <= count, top, jnp.inf)
            expd = jnp.exp2((s_buf[at, :] - shift) * to_exp2)
            s_buf[at, :] = expd
            part = fold(jnp.add, expd)
            total = part if total is None else total + part
        inverse = 1.0 / jnp.sum(total, axis=0, keepdims=True)
        delta = None
        for at in tiles:
            weights_b = (s_buf[at, :] * inverse).astype(BF)
            w_buf[at, :] = weights_b
            part = fold(jnp.add, weights_b.astype(F32) * g_buf[at, :])
            delta = part if delta is None else delta + part
        delta = jnp.sum(delta, axis=0, keepdims=True)
        for at in tiles:
            d_buf[at, :] = (s_buf[at, :] * inverse * (g_buf[at, :] - delta)).astype(BF)

    def gradients(p, n, w_buf, d_buf):
        at = place_of(p)
        grad_scores = d_buf[:n * BLK, :]
        dk = dot(grad_scores, own(at, 0), NN)
        dv = dot(w_buf[:n * BLK, :], own(at, 3), NN)
        for s in range(n):
            for c, code in enumerate(of_slot(at, s)):
                block = code >> 16
                part = (slice(s * BLK, (s + 1) * BLK), slice(c * HEAD, (c + 1) * HEAD))
                dk_ref[block] += dk[part]
                dv_ref[block] += dv[part]
        dq = dot(grad_scores, gathered(at, 1, n), TN)
        for c, (d, half) in enumerate(at):
            part = dq[c * BLK:(c + 1) * BLK, c * HEAD:(c + 1) * HEAD]
            dq_ref[2 * d + half] = (part * scale).astype(BF)

    def step(p, c, n):
        gradients(p - 2, n, w_bufs[c], d_bufs[c])
        products(jnp.minimum(p, pairs - 1), n, s_bufs[c], g_bufs[c])
        softmax(
            jnp.minimum(p - 1, pairs - 1), n, s_bufs[1 - c], g_bufs[1 - c], w_bufs[1 - c], d_bufs[1 - c]
        )

    products(0, slots, s_bufs[0], g_bufs[0])
    products(1, slots, s_bufs[1], g_bufs[1])
    softmax(0, slots, s_bufs[0], g_bufs[0], w_bufs[0], d_bufs[0])
    first, last = 1, pairs // 2 + 1
    for n in range(slots, least, -1):

        def body(i, carry, n=n):
            step(2 * i, 0, n)
            step(2 * i + 1, 1, n)
            return carry

        until = last
        if n > least + 1:
            until = jnp.minimum(1 + ((above[n - 2] + 3) >> 2), last)
        lax.fori_loop(first, until, body, 0)
        first = until

    chunk = blocks // CHUNKS
    copies = []
    for start in range(0, blocks, chunk):

        def finish(b, carry):
            first = pl.multiple_of((b & 1) * BLK, BLK)
            out_ref[b >> 1, pl.ds(first, BLK), :] = (dk_ref[b] * scale).astype(BF)
            out_ref[b >> 1, pl.ds(2 * BLK + first, BLK), :] = dv_ref[b].astype(BF)
            return carry

        lax.fori_loop(start, start + chunk, finish, 0, unroll=4)
        at = pl.ds(start // 2, chunk // 2)
        copies.append(
            pltpu.make_async_copy(out_ref.at[at], out_hbm.at[at], sems.at[3 + start // chunk])
        )
        copies[-1].start()
    copies.append(pltpu.make_async_copy(dq_ref, dq_hbm, sems.at[3 + CHUNKS]))
    copies[-1].start()
    for copy in copies:
        copy.wait()


def attention(states, rows, slots):
    pairs = states.shape[0]
    blocks = pairs * rows // BLK
    tiles = (4 * rows + META) // TILE
    wide = (slots * BLK, 2 * BLK)
    out_shape = [
        jax.ShapeDtypeStruct((pairs, 2 * rows, HEAD), BF),
        jax.ShapeDtypeStruct((blocks, BLK, HEAD), BF),
    ]
    grads, dq = pl.pallas_call(
        functools.partial(attention_kernel, slots=slots),
        in_specs=[pl.BlockSpec(memory_space=pl.ANY)],
        out_specs=[pl.BlockSpec(memory_space=pl.ANY)] * 2,
        out_shape=out_shape,
        scratch_shapes=[pltpu.VMEM((pairs, tiles, TILE, HEAD), BF)]
        + [pltpu.VMEM(out.shape, BF) for out in out_shape]
        + [pltpu.VMEM((blocks, BLK, HEAD), F32)] * 2
        + [
            pltpu.VMEM((pairs, META, HEAD), BF),
            pltpu.VMEM((pairs, HEAD), jnp.int32),
            pltpu.SMEM((pairs, HEAD), jnp.int32),
            pltpu.SMEM((LIST,), jnp.int32),
            pltpu.SMEM((blocks,), jnp.int32),
            pltpu.SemaphoreType.DMA((4 + CHUNKS,)),
        ]
        + [pltpu.VMEM(wide, F32)] * 4
        + [pltpu.VMEM(wide, BF)] * 4,
        compiler_params=pltpu.CompilerParams(vmem_limit_bytes=VMEM_ALL),
        cost_estimate=pl.CostEstimate(
            flops=20 * blocks * slots * BLK * BLK * HEAD,
            bytes_accessed=2 * states.size + 6 * blocks * BLK * HEAD,
            transcendentals=blocks * slots * BLK * BLK,
        ),
        name="attention",
    )(states.reshape(pairs, -1, TILE, HEAD))
    return grads, dq.reshape(pairs, rows, HEAD)


def down_kernel(grads_ref, up_ref, x_ref, out_ref):
    heads = grads_ref.shape[0]
    rows = x_ref.shape[0]
    low = []
    for t in range(2):
        part = slice(t * rows, (t + 1) * rows)
        full = jnp.concatenate([grads_ref[h, part, :] for h in range(heads)], axis=1)
        low.append(dot(full, up_ref[t], NT))
    back_low = jnp.concatenate(low, axis=1).astype(BF)
    terms = dot(back_low, x_ref[...], TN).astype(BF)
    for h in range(heads):
        out_ref[h] = terms[:, h * HEAD:(h + 1) * HEAD]


def down_terms(grads, adapter_up, x):
    rows, feats = x.shape
    return pl.pallas_call(
        down_kernel,
        in_specs=[pl.BlockSpec(memory_space=pltpu.VMEM)] * 3,
        out_specs=pl.BlockSpec(memory_space=pltpu.VMEM),
        out_shape=jax.ShapeDtypeStruct((grads.shape[0], 2 * adapter_up.shape[1], HEAD), BF),
        compiler_params=pltpu.CompilerParams(vmem_limit_bytes=VMEM_SOME),
        cost_estimate=pl.CostEstimate(
            flops=8 * rows * feats * adapter_up.shape[1],
            bytes_accessed=12 * rows * feats,
            transcendentals=0,
        ),
        name="down_terms",
    )(grads, adapter_up, x)


def unpack_kernel(grads_hbm, *refs):
    parts = (len(refs) - 2) // 2
    outs, bufs, grads_ref, sems = refs[:parts], refs[parts:2 * parts], refs[-2], refs[-1]
    heads, all_rows, _ = grads_ref.shape
    rows = all_rows // parts
    here = heads // CHUNKS
    reads = []
    for i in range(CHUNKS):
        at = pl.ds(i * here, here)
        reads.append(
            pltpu.make_async_copy(
                grads_hbm.at[at, pl.ds(0, all_rows)], grads_ref.at[at], sems.at[i]
            )
        )
        reads[-1].start()
    writes = []
    for i in range(CHUNKS):
        reads[i].wait()
        for t in range(parts):
            for h in range(i * here, (i + 1) * here):
                bufs[t][:, h * HEAD:(h + 1) * HEAD] = grads_ref[h, t * rows:(t + 1) * rows, :]
            at = (slice(None), pl.ds(i * here * HEAD, here * HEAD))
            sem = sems.at[CHUNKS + i * parts + t]
            writes.append(pltpu.make_async_copy(bufs[t].at[at], outs[t].at[at], sem))
            writes[-1].start()
    for write in writes:
        write.wait()


def unpack(grads, rows, parts):
    heads = grads.shape[0]
    out = (rows, heads * HEAD)
    return pl.pallas_call(
        unpack_kernel,
        in_specs=[pl.BlockSpec(memory_space=pl.ANY)],
        out_specs=[pl.BlockSpec(memory_space=pl.ANY)] * parts,
        out_shape=[jax.ShapeDtypeStruct(out, BF)] * parts,
        scratch_shapes=[pltpu.VMEM(out, BF)] * parts
        + [
            pltpu.VMEM((heads, parts * rows, HEAD), BF),
            pltpu.SemaphoreType.DMA((CHUNKS * (1 + parts),)),
        ],
        compiler_params=pltpu.CompilerParams(vmem_limit_bytes=VMEM_SOME),
        cost_estimate=pl.CostEstimate(
            flops=0, bytes_accessed=4 * parts * rows * heads * HEAD, transcendentals=0
        ),
        name="unpack",
    )(grads)


def swap(x, axis):
    return lax.all_to_all(x, axis, split_axis=0, concat_axis=0, tiled=True)


def sum_windows(x, first=F32):
    n = lax.axis_size("dp")
    if n % 8 or n > 8:
        step = 1
        while step < n:
            x = x + lax.ppermute(x, "dp", [(i, i ^ step) for i in range(n)])
            step *= 2
        return x
    if first == BF:
        x = lax.reduce_precision(x, exponent_bits=8, mantissa_bits=7)
    near = [
        lax.ppermute(x.astype(first), "dp", [(i, i ^ step) for i in range(n)]).astype(F32)
        for step in (1, 2, 3)
    ]
    x = (x + near[0]) + (near[1] + near[2])
    return x + lax.ppermute(x, "dp", [(i, (i + (2 if i % 4 >= 2 else -2)) % n) for i in range(n)])


def shards(
    features,
    query_states,
    key_states,
    value_states,
    cotangent,
    adapter_down,
    adapter_up,
    block_lists,
    block_counts,
):
    zones = lax.axis_size("zone")
    windows = lax.axis_size("dp")
    rows = query_states.shape[1]
    rank = adapter_down.shape[1]
    all_rows = zones * rows
    x = features[0]

    states = swap(
        pack(
            block_lists[0],
            block_counts,
            query_states[0],
            key_states[0],
            value_states[0],
            cotangent[0],
            x,
            adapter_down.reshape(2 * rank, -1),
        ),
        "zone",
    )
    grads, dq = attention(states, rows, block_lists.shape[2] + 1)
    home = swap(grads, "zone")

    own = states[:, 4 * rows + META:]
    other = lax.ppermute(own, "zone", [(i, i ^ 1) for i in range(zones)])
    parity = (lax.axis_index("zone") & 1).astype(jnp.int32).reshape(1)
    up = sum_windows(up_terms(parity, own, other, grads))

    terms, up = lax.optimization_barrier((down_terms(home, adapter_up, x), up))
    terms = swap(terms, "zone")
    key_grad, value_grad = unpack(home, rows, 2)
    dq, terms, key_grad, value_grad = lax.optimization_barrier((dq, terms, key_grad, value_grad))
    dq = swap(dq, "zone")
    down = sum_windows(jnp.sum(terms.astype(F32), axis=0), BF)
    (query_grad,) = unpack(dq, rows, 1)
    factor = 1.0 / math.sqrt(windows * all_rows)
    return (
        query_grad[None],
        key_grad[None],
        value_grad[None],
        down.reshape(2, rank, HEAD) * factor,
        up.reshape(2, rank, HEAD) * factor,
    )


def solution(mesh):
    rows = P("dp", "zone", None)
    cols = P(None, None, "zone")
    in_specs = (rows, rows, rows, rows, rows, P(), P(), rows, P("dp", "zone"))
    out_specs = (rows, rows, rows, cols, cols)
    return jax.shard_map(shards, mesh=mesh, in_specs=in_specs, out_specs=out_specs, check_vma=False)
```

```python
import functools
import math

import jax
import jax.numpy as jnp
from jax import lax
from jax.experimental import pallas as pl
from jax.experimental.pallas import tpu as pltpu
from jax.sharding import PartitionSpec as P

HEAD = 128
BLK = 64
VMEM_ALL = 63 << 20
VMEM_SOME = 12 << 20
TILE = 16
LIST = 16
META = 16
CHUNKS = 4
PACK_CHUNKS = 2
BF = jnp.bfloat16
F32 = jnp.float32
NT = (((1,), (1,)), ((), ()))
TN = (((0,), (0,)), ((), ()))
NN = (((1,), (0,)), ((), ()))


def dot(a, b, dims):
    return lax.dot_general(a, b, dims, preferred_element_type=F32)


def whole(shape, space=pltpu.VMEM):
    return pl.BlockSpec(memory_space=space)


def pack_kernel(lists_ref, counts_ref, *refs):
    ins, (x_hbm, down_hbm, out_hbm), refs = refs[:4], refs[4:7], refs[7:]
    bufs, (x_ref, down_ref, out_ref, sems) = refs[:4], refs[4:]
    rows, feats = bufs[0].shape
    heads = feats // HEAD
    chunk = feats // PACK_CHUNKS
    states_rows = 4 * rows + META
    reads = []
    for i in range(PACK_CHUNKS):
        at = (slice(None), pl.ds(i * chunk, chunk))
        for t in range(4):
            reads.append(
                pltpu.make_async_copy(ins[t].at[at], bufs[t].at[at], sems.at[i * 4 + t])
            )
            reads[-1].start()
    last = 5 * PACK_CHUNKS
    others = [
        pltpu.make_async_copy(x_hbm, x_ref, sems.at[last]),
        pltpu.make_async_copy(down_hbm, down_ref, sems.at[last + 1]),
    ]
    for read in others:
        read.start()
    blocks, nbr = lists_ref.shape
    row = lax.broadcasted_iota(jnp.int32, (META, HEAD), 0)
    lane = lax.broadcasted_iota(jnp.int32, (META, HEAD), 1)
    meta = jnp.zeros((META, HEAD), jnp.int32)
    for b in range(blocks):
        for n in range(nbr + 1):
            value = lists_ref[b, n - 1] if n else counts_ref[0, b]
            meta = jnp.where((row == 0) & (lane == b * LIST + n), value, meta)
    meta = meta.astype(F32).astype(BF)
    writes = []
    for i in range(PACK_CHUNKS):
        for t in range(4):
            reads[i * 4 + t].wait()
        here = heads // PACK_CHUNKS
        for j in range(i * here, (i + 1) * here):
            cols = slice(j * HEAD, (j + 1) * HEAD)
            for t in range(4):
                out_ref[j, t * rows:(t + 1) * rows, :] = bufs[t][:, cols]
            out_ref[j, 4 * rows:states_rows, :] = meta
        at = (pl.ds(i * here, here), pl.ds(0, states_rows))
        writes.append(pltpu.make_async_copy(out_ref.at[at], out_hbm.at[at], sems.at[4 * PACK_CHUNKS + i]))
        writes[-1].start()
    for read in others:
        read.wait()
    low = dot(x_ref[...], down_ref[...], NT).astype(BF)
    half, rank = rows // 2, low.shape[1] // 2
    for t in range(2):
        part = low[:, t * rank:(t + 1) * rank]
        part = jnp.concatenate([part[:half], part[half:]], axis=1)
        for j in range(t, heads, 2):
            out_ref[j, states_rows:, :] = part
    at = (slice(None), pl.ds(states_rows, half))
    writes.append(pltpu.make_async_copy(out_ref.at[at], out_hbm.at[at], sems.at[last]))
    writes[-1].start()
    for write in writes:
        write.wait()


def pack(lists, counts, q, k, v, g, x, down):
    rows, feats = q.shape
    out = (feats // HEAD, 4 * rows + META + rows // 2, HEAD)
    return pl.pallas_call(
        pack_kernel,
        in_specs=[pl.BlockSpec(memory_space=pltpu.SMEM)] * 2
        + [pl.BlockSpec(memory_space=pl.ANY)] * 6,
        out_specs=pl.BlockSpec(memory_space=pl.ANY),
        out_shape=jax.ShapeDtypeStruct(out, BF),
        scratch_shapes=[pltpu.VMEM((rows, feats), BF)] * 5
        + [
            pltpu.VMEM(down.shape, BF),
            pltpu.VMEM(out, BF),
            pltpu.SemaphoreType.DMA((5 * PACK_CHUNKS + 2,)),
        ],
        compiler_params=pltpu.CompilerParams(vmem_limit_bytes=VMEM_ALL),
        cost_estimate=pl.CostEstimate(flops=0, bytes_accessed=16 * rows * feats, transcendentals=0),
        name="pack",
    )(lists, counts, q, k, v, g, x, down)


def up_kernel(parity_ref, own_ref, other_ref, grads_ref, out_ref):
    parts, half, lanes = own_ref.shape
    rank = lanes // 2
    mine, other = own_ref[...], other_ref[...]
    for t in range(2):
        low = jnp.where(parity_ref[0] == t, mine, other).reshape(parts * half, lanes)
        first = 2 * t * half
        grads = jnp.concatenate(
            [
                grads_ref[:, first:first + half, :].reshape(parts * half, HEAD),
                grads_ref[:, first + half:first + 2 * half, :].reshape(parts * half, HEAD),
            ],
            axis=1,
        )
        both = dot(low, grads, TN)
        out_ref[t * rank:(t + 1) * rank, :] = both[:rank, :HEAD] + both[rank:, HEAD:]


def up_terms(parity, own, other, grads):
    lanes = own.shape[2]
    return pl.pallas_call(
        up_kernel,
        in_specs=[pl.BlockSpec(memory_space=pltpu.SMEM)]
        + [pl.BlockSpec(memory_space=pltpu.VMEM)] * 3,
        out_specs=pl.BlockSpec(memory_space=pltpu.VMEM),
        out_shape=jax.ShapeDtypeStruct((lanes, HEAD), F32),
        compiler_params=pltpu.CompilerParams(vmem_limit_bytes=VMEM_SOME),
        cost_estimate=pl.CostEstimate(
            flops=4 * own.size * HEAD * 2, bytes_accessed=4 * own.size + 2 * grads.size, transcendentals=0
        ),
        name="up_terms",
    )(parity, own, other, grads)


def blockdiag(x):
    zero = jnp.zeros((BLK, HEAD), BF)
    upper = jnp.concatenate([x[:BLK], zero], axis=1)
    lower = jnp.concatenate([zero, x[BLK:]], axis=1)
    return jnp.concatenate([upper, lower], axis=0)


def attention_kernel(
    states_hbm,
    out_hbm,
    dq_hbm,
    states_ref,
    out_ref,
    dq_ref,
    dk_ref,
    dv_ref,
    meta_ref,
    codes_ref,
    ids_ref,
    offset_ref,
    order_ref,
    sems,
    *scratch,
    slots,
):
    blocks = dk_ref.shape[0]
    pairs = blocks // 2
    stride = states_ref.shape[1]
    block_tiles = BLK // TILE
    part_tiles = 2 * block_tiles
    least = 2
    scale = HEAD ** (-0.5)
    to_exp2 = scale * math.log2(math.e)
    s_bufs, g_bufs, w_bufs, d_bufs = (scratch[2 * i:2 * i + 2] for i in range(4))
    first_half = lax.broadcasted_iota(jnp.int32, (1, 2 * BLK), 1) < BLK

    copy_meta = pltpu.make_async_copy(states_hbm.at[:, stride - 1], meta_ref, sems.at[0])
    copy_meta.start()
    copy_states = pltpu.make_async_copy(states_hbm.at[:, pl.ds(0, stride)], states_ref, sems.at[1])
    copy_states.start()
    dk_ref[...] = jnp.zeros_like(dk_ref)

    copy_meta.wait()
    info = jnp.sum(meta_ref[...].astype(F32), axis=1).astype(jnp.int32)
    lane = lax.broadcasted_iota(jnp.int32, info.shape, 1)
    row = lax.broadcasted_iota(jnp.int32, info.shape, 0)
    second = lane >= LIST
    counts = [info[:, c * LIST:c * LIST + 1] for c in range(2)]
    count = jnp.where(second, counts[1], counts[0])
    slot = lane & (LIST - 1)
    ids = jnp.where((slot >= 1) & (slot <= count), info, 2 * row + jnp.where(second, 1, 0))
    codes = (ids >> 1) * stride + (ids & 1) * block_tiles | (ids << 16)
    for c in range(2):
        codes = jnp.where(lane == 2 * LIST + c, counts[c], codes)
    codes_ref[...] = codes
    copy_codes = pltpu.make_async_copy(codes_ref, ids_ref, sems.at[2])
    copy_codes.start()
    dv_ref[...] = jnp.zeros_like(dv_ref)
    copy_codes.wait()

    def count_of(b):
        return ids_ref[b // 2, 2 * LIST + b % 2]

    for c in range(slots + 1):
        offset_ref[c] = 0
    for b in range(blocks):
        n = count_of(b)
        offset_ref[n] = offset_ref[n] + 1
    above = [None] * (slots + 1)
    total = 0
    for c in range(slots - 1, least - 1, -1):
        above[c] = total
        total = total + offset_ref[c]
        offset_ref[c] = above[c]
    for b in range(blocks):
        n = count_of(b)
        place = offset_ref[n]
        offset_ref[n] = place + 1
        order_ref[place] = b
    copy_states.wait()

    flat_ref = states_ref.reshape(pairs * stride, TILE, HEAD)

    def load(first, tiles):
        return flat_ref[pl.ds(first, tiles)].reshape(tiles * TILE, HEAD)

    def place_of(p):
        return [(b >> 1, b & 1) for b in (order_ref[2 * p + c] for c in range(2))]

    def of_slot(at, s):
        return [ids_ref[d, c * LIST + s] for d, c in at]

    def own(at, part):
        tiles = [load(d * stride + c * block_tiles + part * part_tiles, block_tiles) for d, c in at]
        return blockdiag(jnp.concatenate(tiles, axis=0))

    def gathered(at, part, n):
        tiles = []
        for s in range(n):
            first = [(code & 0xFFFF) + part * part_tiles for code in of_slot(at, s)]
            tiles.append(jnp.concatenate([load(f, block_tiles) for f in first], axis=1))
        return jnp.concatenate(tiles, axis=0)

    def products(p, n, s_buf, g_buf):
        at = place_of(p)
        s_buf[:n * BLK, :] = dot(gathered(at, 1, n), own(at, 0), NT)
        g_buf[:n * BLK, :] = dot(gathered(at, 2, n), own(at, 3), NT)

    def softmax(p, n, s_buf, g_buf, w_buf, d_buf):
        used = [ids_ref[d, 2 * LIST + c] for d, c in place_of(p)]
        count = jnp.where(first_half, used[0], used[1])
        tiles = [slice(s * BLK, (s + 1) * BLK) for s in range(n)]

        def fold(op, x):
            return functools.reduce(op, [x[r:r + 8] for r in range(0, BLK, 8)])

        top = None
        for s, at in enumerate(tiles):
            part = fold(jnp.maximum, s_buf[at, :])
            part = part if s <= least else jnp.where(s <= count, part, -jnp.inf)
            top = part if top is None else jnp.maximum(top, part)
        top = jnp.max(top, axis=0, keepdims=True)
        total = None
        for s, at in enumerate(tiles):
            shift = top if s <= least else jnp.where(s <= count, top, jnp.inf)
            expd = jnp.exp2((s_buf[at, :] - shift) * to_exp2)
            s_buf[at, :] = expd
            part = fold(jnp.add, expd)
            total = part if total is None else total + part
        inverse = 1.0 / jnp.sum(total, axis=0, keepdims=True)
        delta = None
        for at in tiles:
            weights_b = (s_buf[at, :] * inverse).astype(BF)
            w_buf[at, :] = weights_b
            part = fold(jnp.add, weights_b.astype(F32) * g_buf[at, :])
            delta = part if delta is None else delta + part
        delta = jnp.sum(delta, axis=0, keepdims=True)
        for at in tiles:
            d_buf[at, :] = (s_buf[at, :] * inverse * (g_buf[at, :] - delta)).astype(BF)

    def gradients(p, n, w_buf, d_buf):
        at = place_of(p)
        grad_scores = d_buf[:n * BLK, :]
        dk = dot(grad_scores, own(at, 0), NN)
        dv = dot(w_buf[:n * BLK, :], own(at, 3), NN)
        for s in range(n):
            for c, code in enumerate(of_slot(at, s)):
                block = code >> 16
                part = (slice(s * BLK, (s + 1) * BLK), slice(c * HEAD, (c + 1) * HEAD))
                dk_ref[block] += dk[part]
                dv_ref[block] += dv[part]
        dq = dot(grad_scores, gathered(at, 1, n), TN)
        for c, (d, half) in enumerate(at):
            part = dq[c * BLK:(c + 1) * BLK, c * HEAD:(c + 1) * HEAD]
            dq_ref[2 * d + half] = (part * scale).astype(BF)

    def step(p, c, n):
        gradients(p - 2, n, w_bufs[c], d_bufs[c])
        products(jnp.minimum(p, pairs - 1), n, s_bufs[c], g_bufs[c])
        softmax(
            jnp.minimum(p - 1, pairs - 1), n, s_bufs[1 - c], g_bufs[1 - c], w_bufs[1 - c], d_bufs[1 - c]
        )

    products(0, slots, s_bufs[0], g_bufs[0])
    products(1, slots, s_bufs[1], g_bufs[1])
    softmax(0, slots, s_bufs[0], g_bufs[0], w_bufs[0], d_bufs[0])
    first, last = 0, pairs // 4
    for n in range(slots, least, -1):

        def body(i, carry, n=n):
            for j in range(4):
                step(4 * i + 2 + j, j % 2, n)
            return carry

        until = last
        if n > least + 1:
            until = (above[n - 2] + 7) >> 3
        lax.fori_loop(first, until, body, 0)
        first = until

    chunk = blocks // CHUNKS
    copies = []
    for start in range(0, blocks, chunk):

        def finish(b, carry):
            first = pl.multiple_of((b & 1) * BLK, BLK)
            out_ref[b >> 1, pl.ds(first, BLK), :] = (dk_ref[b] * scale).astype(BF)
            out_ref[b >> 1, pl.ds(2 * BLK + first, BLK), :] = dv_ref[b].astype(BF)
            return carry

        lax.fori_loop(start, start + chunk, finish, 0, unroll=4)
        at = pl.ds(start // 2, chunk // 2)
        copies.append(
            pltpu.make_async_copy(out_ref.at[at], out_hbm.at[at], sems.at[3 + start // chunk])
        )
        copies[-1].start()
    copies.append(pltpu.make_async_copy(dq_ref, dq_hbm, sems.at[3 + CHUNKS]))
    copies[-1].start()
    for copy in copies:
        copy.wait()


def attention(states, rows, slots):
    pairs = states.shape[0]
    blocks = pairs * rows // BLK
    tiles = (4 * rows + META) // TILE
    wide = (slots * BLK, 2 * BLK)
    out_shape = [
        jax.ShapeDtypeStruct((pairs, 2 * rows, HEAD), BF),
        jax.ShapeDtypeStruct((blocks, BLK, HEAD), BF),
    ]
    grads, dq = pl.pallas_call(
        functools.partial(attention_kernel, slots=slots),
        in_specs=[pl.BlockSpec(memory_space=pl.ANY)],
        out_specs=[pl.BlockSpec(memory_space=pl.ANY)] * 2,
        out_shape=out_shape,
        scratch_shapes=[pltpu.VMEM((pairs, tiles, TILE, HEAD), BF)]
        + [pltpu.VMEM(out.shape, BF) for out in out_shape]
        + [pltpu.VMEM((blocks, BLK, HEAD), F32)] * 2
        + [
            pltpu.VMEM((pairs, META, HEAD), BF),
            pltpu.VMEM((pairs, HEAD), jnp.int32),
            pltpu.SMEM((pairs, HEAD), jnp.int32),
            pltpu.SMEM((LIST,), jnp.int32),
            pltpu.SMEM((blocks,), jnp.int32),
            pltpu.SemaphoreType.DMA((4 + CHUNKS,)),
        ]
        + [pltpu.VMEM(wide, F32)] * 4
        + [pltpu.VMEM(wide, BF)] * 4,
        compiler_params=pltpu.CompilerParams(vmem_limit_bytes=VMEM_ALL),
        cost_estimate=pl.CostEstimate(
            flops=20 * blocks * slots * BLK * BLK * HEAD,
            bytes_accessed=2 * states.size + 6 * blocks * BLK * HEAD,
            transcendentals=blocks * slots * BLK * BLK,
        ),
        name="attention",
    )(states.reshape(pairs, -1, TILE, HEAD))
    return grads, dq.reshape(pairs, rows, HEAD)


def down_kernel(grads_ref, up_ref, x_ref, out_ref):
    heads = grads_ref.shape[0]
    rows = x_ref.shape[0]
    low = []
    for t in range(2):
        part = slice(t * rows, (t + 1) * rows)
        full = jnp.concatenate([grads_ref[h, part, :] for h in range(heads)], axis=1)
        low.append(dot(full, up_ref[t], NT))
    back_low = jnp.concatenate(low, axis=1).astype(BF)
    terms = dot(back_low, x_ref[...], TN).astype(BF)
    for h in range(heads):
        out_ref[h] = terms[:, h * HEAD:(h + 1) * HEAD]


def down_terms(grads, adapter_up, x):
    rows, feats = x.shape
    return pl.pallas_call(
        down_kernel,
        in_specs=[pl.BlockSpec(memory_space=pltpu.VMEM)] * 3,
        out_specs=pl.BlockSpec(memory_space=pltpu.VMEM),
        out_shape=jax.ShapeDtypeStruct((grads.shape[0], 2 * adapter_up.shape[1], HEAD), BF),
        compiler_params=pltpu.CompilerParams(vmem_limit_bytes=VMEM_SOME),
        cost_estimate=pl.CostEstimate(
            flops=8 * rows * feats * adapter_up.shape[1],
            bytes_accessed=12 * rows * feats,
            transcendentals=0,
        ),
        name="down_terms",
    )(grads, adapter_up, x)


def unpack_kernel(grads_hbm, *refs):
    parts = (len(refs) - 2) // 2
    outs, bufs, grads_ref, sems = refs[:parts], refs[parts:2 * parts], refs[-2], refs[-1]
    heads, all_rows, _ = grads_ref.shape
    rows = all_rows // parts
    here = heads // CHUNKS
    reads = []
    for i in range(CHUNKS):
        at = pl.ds(i * here, here)
        reads.append(
            pltpu.make_async_copy(
                grads_hbm.at[at, pl.ds(0, all_rows)], grads_ref.at[at], sems.at[i]
            )
        )
        reads[-1].start()
    writes = []
    for i in range(CHUNKS):
        reads[i].wait()
        for t in range(parts):
            for h in range(i * here, (i + 1) * here):
                bufs[t][:, h * HEAD:(h + 1) * HEAD] = grads_ref[h, t * rows:(t + 1) * rows, :]
            at = (slice(None), pl.ds(i * here * HEAD, here * HEAD))
            sem = sems.at[CHUNKS + i * parts + t]
            writes.append(pltpu.make_async_copy(bufs[t].at[at], outs[t].at[at], sem))
            writes[-1].start()
    for write in writes:
        write.wait()


def unpack(grads, rows, parts):
    heads = grads.shape[0]
    out = (rows, heads * HEAD)
    return pl.pallas_call(
        unpack_kernel,
        in_specs=[pl.BlockSpec(memory_space=pl.ANY)],
        out_specs=[pl.BlockSpec(memory_space=pl.ANY)] * parts,
        out_shape=[jax.ShapeDtypeStruct(out, BF)] * parts,
        scratch_shapes=[pltpu.VMEM(out, BF)] * parts
        + [
            pltpu.VMEM((heads, parts * rows, HEAD), BF),
            pltpu.SemaphoreType.DMA((CHUNKS * (1 + parts),)),
        ],
        compiler_params=pltpu.CompilerParams(vmem_limit_bytes=VMEM_SOME),
        cost_estimate=pl.CostEstimate(
            flops=0, bytes_accessed=4 * parts * rows * heads * HEAD, transcendentals=0
        ),
        name="unpack",
    )(grads)


def swap(x, axis):
    return lax.all_to_all(x, axis, split_axis=0, concat_axis=0, tiled=True)


def sum_windows(x, first=F32):
    n = lax.axis_size("dp")
    if n % 8 or n > 8:
        step = 1
        while step < n:
            x = x + lax.ppermute(x, "dp", [(i, i ^ step) for i in range(n)])
            step *= 2
        return x
    if first == BF:
        x = lax.reduce_precision(x, exponent_bits=8, mantissa_bits=7)
    near = [
        lax.ppermute(x.astype(first), "dp", [(i, i ^ step) for i in range(n)]).astype(F32)
        for step in (1, 2, 3)
    ]
    x = (x + near[0]) + (near[1] + near[2])
    return x + lax.ppermute(x, "dp", [(i, (i + (2 if i % 4 >= 2 else -2)) % n) for i in range(n)])


def shards(
    features,
    query_states,
    key_states,
    value_states,
    cotangent,
    adapter_down,
    adapter_up,
    block_lists,
    block_counts,
):
    zones = lax.axis_size("zone")
    windows = lax.axis_size("dp")
    rows = query_states.shape[1]
    rank = adapter_down.shape[1]
    all_rows = zones * rows
    x = features[0]

    states = swap(
        pack(
            block_lists[0],
            block_counts,
            query_states[0],
            key_states[0],
            value_states[0],
            cotangent[0],
            x,
            adapter_down.reshape(2 * rank, -1),
        ),
        "zone",
    )
    grads, dq = attention(states, rows, block_lists.shape[2] + 1)
    home = swap(grads, "zone")

    own = states[:, 4 * rows + META:]
    other = lax.ppermute(own, "zone", [(i, i ^ 1) for i in range(zones)])
    parity = (lax.axis_index("zone") & 1).astype(jnp.int32).reshape(1)
    up = sum_windows(up_terms(parity, own, other, grads))

    terms, up = lax.optimization_barrier((down_terms(home, adapter_up, x), up))
    terms = swap(terms, "zone")
    key_grad, value_grad = unpack(home, rows, 2)
    dq, terms, key_grad, value_grad = lax.optimization_barrier((dq, terms, key_grad, value_grad))
    dq = swap(dq, "zone")
    down = sum_windows(jnp.sum(terms.astype(F32), axis=0), BF)
    (query_grad,) = unpack(dq, rows, 1)
    factor = 1.0 / math.sqrt(windows * all_rows)
    return (
        query_grad[None],
        key_grad[None],
        value_grad[None],
        down.reshape(2, rank, HEAD) * factor,
        up.reshape(2, rank, HEAD) * factor,
    )


def solution(mesh):
    rows = P("dp", "zone", None)
    cols = P(None, None, "zone")
    in_specs = (rows, rows, rows, rows, rows, P(), P(), rows, P("dp", "zone"))
    out_specs = (rows, rows, rows, cols, cols)
    return jax.shard_map(shards, mesh=mesh, in_specs=in_specs, out_specs=out_specs, check_vma=False)
```
